32 devices in a mesh: front: 8 (over y, x, core), blk: 4 (over z).
Axes of the slice: x: 2, y: 2, z: 4, core: 2. Of those that a mesh axis runs over, the one named last changes fastest.
Arguments:
- child_diag: float32 [8192, 1024], P(('front', 'blk')), as said below
- child_top: float32 [4096, 1024], P(('front', 'blk')), may hold values from -0.078125 to 0.078125
- child_rows: float32 [16384, 1024], P(('front', 'blk')), may hold values from -12 to 12
- row_owner: int32 [8, 16, 1], P('front'), may hold values from 0 to 7; in each aligned block of 16 rows (0 to 15, 16 to 31, ..., all dimensions but the last counted through in order) at most 4 rows name the same one
- row_slot: int32 [8, 16], P('front'), may hold values from 0 to 3
- col_block: int32 [8, 4], P('front'), may hold values from 0 to 1
- parent_diag: float32 [1024, 1024], P('blk'), as said below
- parent_rows: float32 [4096, 1024], P('front', 'blk'), may hold values from -6 to 6
Outputs:
- parent_factor: float32 [1024, 1024], P('blk')
- parent_panel: float32 [4096, 1024], P(('front', 'blk'))
The draws below stay inside these ranges and needn't reach their ends.
Inputs may be any that keep to these rules, and one draw needn't show every extreme that they name: `row_owner`: within the 16 row blocks of one child no owner is named more than 4 times, and in some children one owner is named exactly 4 times. `child_diag`: each 1024 x 1024 block is symmetric with all eigenvalues at least 1. `parent_diag`: symmetric with all eigenvalues at least 24; parent_diag - diag_update has all eigenvalues at least 12.
All inputs are finite; a program needn't handle non-finite values.
Results may differ from the reference program's by a relative error of at most 0.0001.
Values sent between devices are 32-bit elements; how exact they have to be, the bound alone decides.
No kernel may reach another device: no remote copies, remote signals or barrier semaphores. Data moves between devices by JAX's collectives and lax.ppermute only.
A program may use at most 192 MiB of HBM per device.

```python
import math
import jax
import jax.numpy as jnp
import numpy as np
from jax import lax

W = 1024
TILE = 128
TA = 4
PB = 4
FRONTS = 8
BLOCKS = 4
CQ = 2
CAP = 4
TOP_ROWS = 4096
CHILD_ROWS = 16384
PARENT_ROWS = 4096
N_FRONT = 8
N_BLK = 4


def gram_blocks(samples, shift):
    product = jnp.einsum('aik,ajk->aij', samples, samples, precision=lax.Precision.HIGHEST) / W
    return product + shift * jnp.eye(W, dtype=jnp.float32)[None]


def draw_child_diag(key, part):
    subkey = jax.random.fold_in(key, 11)
    samples = jax.random.truncated_normal(subkey, -6.0, 6.0, (FRONTS, W, W), jnp.float32)
    return gram_blocks(samples, 1.0).reshape(FRONTS * W, W)


def draw_parent_diag(key, part):
    subkey = jax.random.fold_in(key, 23)
    samples = jax.random.truncated_normal(subkey, -6.0, 6.0, (1, W, W), jnp.float32)
    return gram_blocks(samples, 24.0).reshape(W, W)


def touch_ends(values, rng, low, top_value):
    shape = values.shape
    place = [jax.random.randint(jax.random.fold_in(rng, axis), (), 0, shape[axis]) for axis in range(len(shape))]
    values = values.at[tuple(place)].set(low)
    longest = shape.index(max(shape))
    place[longest] = (place[longest] + 1) % shape[longest]
    return values.at[tuple(place)].set(top_value)


def level_of(rng, extent, shards, smallest, largest):
    level, own = 1.0, jax.random.fold_in(rng, 6)
    for dim, parts in shards:
        steps = jnp.exp(jax.random.uniform(jax.random.fold_in(own, dim), (parts,), jnp.float32, smallest / len(shards), largest / len(shards)))
        level = level * jnp.repeat(steps, extent[dim] // parts).reshape([-1 if axis == dim else 1 for axis in range(len(extent))])
    return level


def shared_out(own_key, own, number, rows, number_of, top, most, skew):
    order = jax.random.permutation(own_key, number_of)
    heavy_load, usual = shares(number_of, rows * top, most, skew, True), shares(number_of, rows * top, most, skew, False)
    places = jnp.arange(number_of)

    def named(lengths, turn):
        used = int((lengths > 0).sum())
        fixed = max(1, used // 4)
        moved = fixed + (places - fixed + turn * (used - fixed)) % max(1, number_of - fixed)
        return jnp.zeros((number_of,), jnp.int32).at[order[jnp.where(places < fixed, places, moved)]].set(jnp.asarray(lengths, jnp.int32))

    lengths = jnp.where(number % 4 == 0, named(heavy_load, number // 4), named(usual, number - number // 4 - 1))
    mixed = jax.random.permutation(jax.random.fold_in(own, 3), number_of)
    giver, taker = mixed[0:number_of // 2 * 2:2], mixed[1:number_of // 2 * 2:2]
    margin = jnp.minimum(lengths[giver] - 1, most - lengths[taker]) // 2
    margin = jnp.where((giver == order[0]) | (taker == order[0]) | (lengths[taker] == 0), 0, jnp.maximum(margin, 0))
    moved = jax.random.randint(jax.random.fold_in(own, 4), (number_of // 2,), 0, 1 << 20) % (margin + 1)
    lengths = lengths.at[giver].add(-moved).at[taker].add(moved)
    members = jnp.searchsorted(jnp.cumsum(lengths), jnp.arange(rows * top), side="right").astype(jnp.int32)
    listing = members.reshape(top, rows).T
    listing = listing[jax.random.permutation(jax.random.fold_in(own, 1), rows)]
    turn = jax.random.randint(jax.random.fold_in(own, 2), (rows, 1), 0, top)
    return jnp.take_along_axis(listing, (jnp.arange(top)[None, :] + turn) % top, axis=1)


def shares(count, total, most, lean, full):
    weights = [(1 << 20) // math.isqrt(rank ** lean) + 1 for rank in range(1, count + 1)]
    largest = most if full else min(most, max(-(-total // count), total * weights[0] // sum(weights)))
    least = 1 if total - largest >= count - 1 else 0
    holding, surplus = [largest] + [least] * (count - 1), total - largest - least * (count - 1)
    while surplus > 0:
        movable = [i for i in range(1, count) if holding[i] < largest] or [i for i in range(1, count) if holding[i] < most]
        pool, left = sum([weights[i] for i in movable]), surplus
        for i in movable:
            addition = min(most - holding[i], max(1, left * weights[i] // pool), surplus)
            holding[i] = holding[i] + addition
            surplus = surplus - addition
    return np.array(holding)


def bell_draw(own_key, extent, width, most, shards=(), kind=jnp.bfloat16):
    entries = jax.random.normal(own_key, extent, jnp.float32) * width
    if len(shards) > 0:
        entries = level_of(own_key, extent, shards, -0.22, 0.18) * entries
    return jnp.clip(entries, min=-most, max=most).astype(kind)


def setup_inputs(seed: int = 0) -> dict:
    keys = jax.random.split(jax.random.key(seed), 9)
    child_diag = draw_child_diag(jax.random.fold_in(keys[8], 71), 0)
    child_top = bell_draw(keys[1], (TOP_ROWS, W), 0.0125, 0.078125, ((0, 32),), jnp.float32)
    child_rows = bell_draw(keys[2], (CHILD_ROWS, W), 2.0, 12.0, ((0, 32),), jnp.float32)
    row_owner_keys = jax.random.split(jax.random.fold_in(keys[3], 1), FRONTS * (BLOCKS * TA) // (BLOCKS * TA))
    row_owner_turns = jax.random.permutation(jax.random.fold_in(keys[3], 3), FRONTS * (BLOCKS * TA) // (BLOCKS * TA))
    row_owner = jax.vmap(lambda own, number: shared_out(jax.random.fold_in(keys[3], 2), own, number, BLOCKS * TA, FRONTS, 1, CAP, 2))(row_owner_keys, row_owner_turns).reshape((FRONTS, BLOCKS * TA, 1))
    row_slot = touch_ends(jax.random.randint(keys[4], (FRONTS, BLOCKS * TA), 0, PB), jax.random.fold_in(keys[4], 1), 0, PB - 1).astype(jnp.int32)
    col_block = touch_ends(jax.random.randint(keys[5], (FRONTS, BLOCKS), 0, CQ), jax.random.fold_in(keys[5], 1), 0, CQ - 1).astype(jnp.int32)
    parent_diag = draw_parent_diag(jax.random.fold_in(keys[8], 71), 0)
    parent_rows = bell_draw(keys[7], (PARENT_ROWS, W), 1.0, 6.0, ((0, 8), (1, 4)), jnp.float32)
    return dict(child_diag=child_diag, child_top=child_top, child_rows=child_rows, row_owner=row_owner, row_slot=row_slot, col_block=col_block, parent_diag=parent_diag, parent_rows=parent_rows)


HIGHEST = lax.Precision.HIGHEST

def right_solve(factor, matrix):
    return jax.scipy.linalg.solve_triangular(factor, matrix.T, lower=True).T

def reference(child_diag, child_top, child_rows, row_owner, row_slot, col_block, parent_diag, parent_rows):
    block_width = W // TILE
    diag_stack = child_diag.reshape(N_FRONT, W, W)
    top_stack = child_top.reshape(N_FRONT, N_BLK * TILE, W)
    rows_stack = child_rows.reshape(N_FRONT, N_BLK * TA * TILE, W)
    targets = (row_owner.reshape(N_FRONT, N_BLK * TA) * PB + row_slot).astype(jnp.int32)
    columns = (jnp.arange(N_BLK, dtype=jnp.int32)[None, :] * CQ + col_block).astype(jnp.int32)

    def one_child(carry, inputs):
        panel_update, diag_update = carry
        diag_block, top_block, rows_block, target_row, column_row = inputs
        factor = jnp.linalg.cholesky(diag_block)
        top_solved = right_solve(factor, top_block)
        rows_solved = right_solve(factor, rows_block)
        schur_tiles = jnp.dot(rows_solved, top_solved.T, precision=HIGHEST)
        schur_tiles = schur_tiles.reshape(N_BLK * TA, TILE, N_BLK, TILE).transpose(0, 2, 1, 3)
        panel_update = panel_update.at[target_row[:, None], :, column_row[None, :], :].add(schur_tiles)
        cross_terms = jnp.dot(top_solved, top_solved.T, precision=HIGHEST)
        cross_terms = cross_terms.reshape(N_BLK, TILE, N_BLK, TILE).transpose(0, 2, 1, 3)
        diag_update = diag_update.at[column_row[:, None], :, column_row[None, :], :].add(cross_terms)
        return ((panel_update, diag_update), None)
    panel_zero = jnp.zeros((N_FRONT * PB, TILE, block_width, TILE), jnp.float32)
    diag_zero = jnp.zeros((block_width, TILE, block_width, TILE), jnp.float32)
    (panel_update, diag_update), unused = lax.scan(one_child, (panel_zero, diag_zero), (diag_stack, top_stack, rows_stack, targets, columns))
    parent_factor = jnp.linalg.cholesky(parent_diag - diag_update.reshape(W, W))
    updated = parent_rows - panel_update.reshape(N_FRONT * PB * TILE, W)
    parent_panel = right_solve(parent_factor, updated)
    return (parent_factor, parent_panel)
```

```python
import math

import jax
import jax.numpy as jnp
from jax import lax
from jax.experimental import pallas as pl
from jax.experimental.pallas import tpu as pltpu
from jax.sharding import PartitionSpec as P

HIGHEST = lax.Precision.HIGHEST
T = 128
S = 32
Q = 256

PLAN = (
    (0, 1, 2, 3, 0, 2, 3, 0, 0, 0),
    (1, 0, 2, 3, 1, 0, 0, 1, 2, 3),
    (2, 3, 1, 0, 2, 1, 0, 2, 3, 3),
    (3, 2, 1, 0, 0, 0, 0, 3, 1, 0),
)
UP = ((0, 1), (1, 2), (2, 3))
DOWN = ((1, 0), (2, 1), (3, 2))
F32 = jnp.float32


def mm(x, y, a, b):
    return lax.dot_general(x, y, (((a,), (b,)), ((), ())), precision=HIGHEST, preferred_element_type=F32)


def mm_nn(x, y):
    return mm(x, y, 1, 0)


def mm_nt(x, y):
    return mm(x, y, 1, 1)


def mm_tn(x, y):
    return mm(x, y, 0, 0)


def call(body, name, out_shape, args, smem, scratch=(), loose=0):
    vm = pl.BlockSpec(memory_space=pltpu.VMEM)
    sm = pl.BlockSpec(memory_space=pltpu.SMEM)
    outs = out_shape if isinstance(out_shape, tuple) else (out_shape,)
    held = [*outs, *args, *[jax.ShapeDtypeStruct(x.shape, x.dtype) for x in scratch]]
    size = sum(4 * math.prod(x.shape) for x in held)
    fixed = smem + loose
    args = [*args[:fixed], *[pltpu.with_memory_space_constraint(x, pltpu.HBM) for x in args[fixed:]]]
    got = pl.pallas_call(
        body,
        in_specs=[sm] * smem + [vm] * (len(args) - smem),
        out_specs=[vm] * len(outs),
        out_shape=[pltpu.HBM(x.shape, x.dtype) for x in outs],
        scratch_shapes=list(scratch),
        compiler_params=pltpu.CompilerParams(vmem_limit_bytes=size + size // 8 + 8 * 1024 * 1024),
        name=name,
    )(*args)
    return tuple(got) if isinstance(out_shape, tuple) else got[0]


def sds(*shape):
    return jax.ShapeDtypeStruct(shape, F32)


def eliminate32(rows, inv_rows, lane0):
    ng = S // 8
    sub = lax.broadcasted_iota(jnp.int32, (8, T), 0)
    xa = [rows[8 * g:8 * g + 8] for g in range(ng)]
    xi = [inv_rows[8 * g:8 * g + 8] for g in range(ng)]
    bc = [
        [None] * (c // 8)
        + [jnp.broadcast_to(xa[g][:, lane0 + c:lane0 + c + 1], (8, T)) for g in range(c // 8, ng)]
        for c in range(S)
    ]

    def row(groups, i):
        return jnp.broadcast_to(groups[i // 8][i % 8:i % 8 + 1], (8, T))

    scale = [jnp.zeros((8, T), F32) for _ in range(ng)]
    for j in range(0, S, 2):
        gj, rj = j // 8, j % 8
        c1, c2 = bc[j], bc[j + 1]
        p11, p21, p22 = row(c1, j), row(c1, j + 1), row(c2, j + 1)
        det = p11 * p22 - p21 * p21
        rd = 1.0 / det
        t1 = [None if g < gj else (c1[g] * p22 - c2[g] * p21) * rd for g in range(ng)]
        t2 = [None if g < gj else (c2[g] * p11 - c1[g] * p21) * rd for g in range(ng)]
        for c in range(j + 2, S):
            m1, m2 = row(c1, c), row(c2, c)
            for g in range(c // 8, ng):
                bc[c][g] = bc[c][g] - (t1[g] * m1 + t2[g] * m2)
        r1 = lax.rsqrt(p11)
        q1 = r1 * r1
        r2 = lax.rsqrt(det * q1)
        scale[gj] = jnp.where(sub == rj, r1, jnp.where(sub == rj + 1, r2, scale[gj]))
        k1, k2 = list(t1), list(t2)
        k1[gj] = jnp.where(sub > rj + 1, t1[gj], jnp.where(sub == rj + 1, p21 * q1, 0.0))
        k2[gj] = jnp.where(sub > rj + 1, t2[gj], 0.0)
        for x in (xa, xi):
            x1, x2 = row(x, j), row(x, j + 1)
            for g in range(gj, ng):
                x[g] = x[g] - (k1[g] * x1 + k2[g] * x2)
    return (
        jnp.concatenate([a * s for a, s in zip(xa, scale)], 0),
        jnp.concatenate([a * s for a, s in zip(xi, scale)], 0),
    )


def split3(x):
    h = x.astype(jnp.bfloat16)
    r = x - h.astype(F32)
    m = r.astype(jnp.bfloat16)
    return h, m, (r - m.astype(F32)).astype(jnp.bfloat16)


def factor128(a):
    r = lax.broadcasted_iota(jnp.int32, (T, T), 0)
    c = lax.broadcasted_iota(jnp.int32, (T, T), 1)
    inv = jnp.where(r == c, 1.0, 0.0).astype(F32)
    us, ls = [], []
    for s in range(T // S):
        u, li = eliminate32(a[:S], inv[:S], s * S)
        us.append(u)
        ls.append(li)
        if s < T // S - 1:
            h, m, l = split3(u)
            hi, mi, lo = split3(li)
            left = jnp.concatenate([h, h, m, h, l, m], 0)
            right = jnp.concatenate([jnp.concatenate([x, y], 1) for x, y in
                                     ((h, hi), (m, mi), (h, hi), (l, lo), (h, hi), (m, mi))], 0)
            both = lax.dot_general(left, right, (((0,), (0,)), ((), ())), preferred_element_type=F32)
            a = a[S:] - both[(s + 1) * S:, :T]
            inv = inv[S:] - both[(s + 1) * S:, T:]
    u = jnp.concatenate(us, 0)
    return jnp.where(c >= r, u, 0.0), jnp.concatenate(ls, 0)


def factor_panel(pan, width, li_ref, u_ref, keep=None):
    def half(i, carry):
        d = pl.ds(pl.multiple_of(i * T, T), T)
        u, li = factor128(pan[d, d])
        li_ref[d, d] = li
        if keep is not None:
            keep[d, d] = u
        @pl.when(i == 0)
        def _():
            u12 = mm_nn(li, pan[:T, T:Q])
            pan[:T, T:Q] = u12
            pan[T:, T:Q] -= mm_tn(u12, u12)
            if keep is not None:
                keep[:T, T:] = u12
                keep[T:, :T] = jnp.zeros((T, T), F32)
        return carry
    lax.fori_loop(0, 2, half, 0)
    li_ref[:T, T:] = jnp.zeros((T, T), F32)
    li_ref[T:, :T] = -mm_nn(li_ref[T:, T:], mm_tn(pan[:T, T:Q], li_ref[:T, :T]))


def spread_panel(pan, width, li_ref, u_ref):
    u_ref[...] = mm_nn(li_ref[...], pan[:, Q:width])


def update_panel(pan, p, us):
    for q in range(p):
        o = (p - q - 1) * Q
        pan[:, :(4 - p) * Q] -= mm_tn(us[q][:, o:o + Q], us[q][:, o:])


def own_stage(info, c_ref, li_ref, u_ref, pan):
    for p in range(4):
        pan[:, p * Q:(p + 1) * Q] = c_ref[:, pl.ds(pl.multiple_of(info[p] * Q, Q), Q)]
    factor_panel(pan, 4 * Q, li_ref, u_ref)
    spread_panel(pan, 4 * Q, li_ref, u_ref)


def next_stage(p, picks):
    count = 1 + max(a for pick in picks for a, _ in pick)
    def body(info, *refs):
        got, us = refs[:count], refs[count:count + p]
        rest = refs[count + p:]
        li_ref, pan = rest[0], rest[-1]
        for z in range(4):
            @pl.when(info[10] == z)
            def _():
                for i, (a, lead) in enumerate(picks[z]):
                    pan[:, i * Q:(i + 1) * Q] = got[a][...] if lead is None else got[a][lead]
        update_panel(pan, p, us)
        factor_panel(pan, (4 - p) * Q, li_ref, None)
        if p < 3:
            spread_panel(pan, (4 - p) * Q, li_ref, rest[1])
    return body


def child_stage(p, info, got, us, picks):
    w = (3 - p) * Q
    out = (sds(Q, Q), sds(Q, w)) if p < 3 else (sds(Q, Q),)
    return call(next_stage(p, picks), "child_panel", out, (info, *got, *us), 1, [vmem(Q, (4 - p) * Q)], len(got))


def solve_rows(read, us, lis, out):
    for p in range(4):
        x = read(p)
        for q in range(p):
            o = (p - q - 1) * Q
            x = x - mm_nn(out[:, q * Q:(q + 1) * Q], us[q][:, o:o + Q])
        out[:, p * Q:(p + 1) * Q] = mm_nt(x, lis[p][...])


def pieces_kernel(info, c_ref, up, down):
    for i in range(3):
        up[i] = c_ref[:, pl.ds(pl.multiple_of(info[4 + i] * Q, Q), Q)]
        down[i] = c_ref[:, pl.ds(pl.multiple_of(info[7 + i] * Q, Q), Q)]


def rows_kernel(p):
    def body(info, r_ref, *refs):
        before, us, li_ref, out = refs[:p], refs[p:2 * p], refs[2 * p], refs[2 * p + 1]
        x = r_ref[:, pl.ds(pl.multiple_of(info[p] * Q, Q), Q)]
        for q in range(p):
            o = (p - q - 1) * Q
            x = x - mm_nn(before[q][...], us[q][:, o:o + Q])
        out[...] = mm_nt(x, li_ref[...])
    return body


def rows_stage(p, info, rows, before, us, li):
    return call(rows_kernel(p), "rows_solved", sds(rows.shape[0], Q), (info, rows, *before, *us, li), 1)


def top_kernel(info, cb, d1, d2, d3, p1, p2, p3, own, u0, u1, u2, l0, l1, l2, l3, out, cross, full):
    z = info[10]
    for ref, shift in ((own, 0), (p1, -1), (p2, -2), (p3, -3), (d1, 1), (d2, 2), (d3, 3)):
        at = z + shift
        @pl.when((at >= 0) & (at < 4))
        def _():
            full[pl.ds(pl.multiple_of(at * T, T), T), :] = ref[...]
    solve_rows(lambda p: full[:, pl.ds(pl.multiple_of(info[p] * Q, Q), Q)], (u0, u1, u2), (l0, l1, l2, l3), out)
    cross[...] = jnp.zeros(cross.shape, F32)
    n1, n2 = lax.rem(z + 1, 4), lax.rem(z + 2, 4)
    a0, a1, a2 = cb[0, z], cb[0, n1], cb[0, n2]
    low = z < 2
    rows = cross.shape[2]
    mine = out[pl.ds(pl.multiple_of(z * T, T), T), :]
    for k, place, take in ((z, 2 * a0, a0 >= 0), (n1, 3 + 2 * a0 + a1, a0 >= 0),
                           (n2, 7 + jnp.where(low, a0, a2), jnp.where(low, 1 - a2, a0) == 1)):
        block = mm_nt(mine, out[pl.ds(pl.multiple_of(k * T, T), T), :])
        @pl.when(take)
        def _():
            for r in range(cross.shape[0]):
                cross[r, place] = block[r * rows:(r + 1) * rows]


def schur_kernel(r0, r1, r2, r3, t_ref, out):
    for k in range(4):
        at = slice(k * T, (k + 1) * T)
        out[k] = sum(mm_nt(r[...], t_ref[at, p * Q:(p + 1) * Q]) for p, r in enumerate((r0, r1, r2, r3)))


def strip_kernel(info, recv, base, out):
    z = info[10]
    n1, n2 = lax.rem(z + 1, 4), lax.rem(z + 2, 4)
    def start(a, k, b):
        return base[a, :, pl.ds(pl.multiple_of(k * Q + b * T, T), T)]
    out[0] = start(0, z, 0)
    out[1] = start(0, z, 1)
    out[2] = start(1, z, 1)
    for a in range(2):
        for b in range(2):
            out[3 + 2 * a + b] = start(a, n1, b)
    @pl.when(z < 2)
    def _():
        out[7] = start(0, n2, 0)
        out[8] = start(1, n2, 0)
    @pl.when(z >= 2)
    def _():
        out[7] = start(1, n2, 0)
        out[8] = start(1, n2, 1)
    total = recv[0]
    for f in range(1, recv.shape[0]):
        total = total + recv[f]
    out[...] = out[...] - total


def nine(z):
    b, n1, n2 = 2 * z, 2 * ((z + 1) % 4), 2 * ((z + 2) % 4)
    places = [(b, b), (b, b + 1), (b + 1, b + 1)]
    places += [(b + i, n1 + j) for i in range(2) for j in range(2)]
    places += [(b, n2), (b + 1, n2)] if z < 2 else [(b + 1, n2), (b + 1, n2 + 1)]
    return [(i, j, False) if i <= j else (j, i, True) for i, j in places]


def parent_first(rels):
    def body(info, *refs):
        got = refs[:max(1, len(rels))]
        l0, keep, rest, u0, pan, tiles = refs[len(got):]
        z, f = info[10], info[11]
        if rels:
            for ref, (fs, z0) in zip(got, rels):
                rows = ref.shape[3]
                for i, rf in enumerate(fs):
                    src = jnp.bitwise_xor(f, rf)
                    for j in range(ref.shape[1]):
                        zz = jnp.bitwise_xor(z, z0 + j)
                        tiles[zz, :, pl.ds(pl.multiple_of(src * rows, rows), rows), :] = ref[i, j]
        else:
            tiles[...] = got[0][...]
        for zz in range(4):
            for i, (r, c, turned) in enumerate(nine(zz)):
                block = tiles[zz, i]
                target, at = (pan, 0) if r < 2 else (rest, 2)
                r, c = r - at, c - at
                target[r * T:(r + 1) * T, c * T:(c + 1) * T] = block.T if turned else block
        pan[T:, :T] = jnp.zeros((T, T), F32)
        for p in range(3):
            rest[(2 * p + 1) * T:(2 * p + 2) * T, 2 * p * T:(2 * p + 1) * T] = jnp.zeros((T, T), F32)
        factor_panel(pan, 4 * Q, l0, None, keep)
        spread_panel(pan, 4 * Q, l0, u0)
    return body


def parent_next(p):
    def body(rest, *refs):
        us, (li, keep, u, pan) = refs[:p], refs[p:]
        pan[...] = rest[(p - 1) * Q:p * Q, (p - 1) * Q:]
        update_panel(pan, p, us)
        factor_panel(pan, (4 - p) * Q, li, None, keep)
        spread_panel(pan, (4 - p) * Q, li, u)
    return body


def parent_last(info, rest, u0, u1, u2, k0, k1, k2, li, own, pan, k3):
    us, keeps = (u0, u1, u2), (k0, k1, k2, k3)
    pan[...] = rest[2 * Q:, 2 * Q:]
    update_panel(pan, 3, us)
    factor_panel(pan, Q, li, None, k3)
    for zz in range(4):
        @pl.when(info[10] == zz)
        def _():
            for q in range(4):
                if q < zz:
                    block = us[q][:, (zz - q - 1) * Q:(zz - q) * Q].T
                elif q == zz:
                    block = keeps[zz][...].T
                else:
                    block = jnp.zeros((Q, Q), F32)
                own[:, q * Q:(q + 1) * Q] = block


def vmem(*shape):
    return pltpu.VMEM(shape, F32)


def panel_kernel(x_ref, u0, u1, u2, l0, l1, l2, l3, out):
    solve_rows(lambda p: x_ref[p], (u0, u1, u2), (l0, l1, l2, l3), out)


def pack_kernel(info, cb, owner, slot, x_ref, out):
    out[...] = jnp.zeros(out.shape, F32)
    def one(b, carry):
        o, at = owner[b], pl.ds(pl.multiple_of(slot[b] * T, T), T)
        out[o, at, :] = out[o, at, :] + x_ref[b]
        return carry
    lax.fori_loop(0, x_ref.shape[0], one, 0)
    out[:, 4 * T:, :] = jnp.full((out.shape[0], 8, T), cb[0, info[10]].astype(F32))


def land_kernel(recv, rows_ref, out):
    for s in range(4):
        at = slice(s * T, (s + 1) * T)
        def one(f, carry):
            right = jnp.broadcast_to(recv[f, 4 * T:4 * T + 1, :], (T, T)) > 0.5
            x = recv[f, at, :]
            return carry[0] - jnp.where(right, 0.0, x), carry[1] - jnp.where(right, x, 0.0)
        out[s, :, :T], out[s, :, T:] = lax.fori_loop(0, recv.shape[0], one, (rows_ref[at, :T], rows_ref[at, T:]))


def swap(x, axis, bit):
    n = lax.axis_size(axis)
    return lax.ppermute(x, axis, [(i, i ^ bit) for i in range(n)])


def everywhere(parts):
    fronts = lax.axis_size("front")
    bits = [1 << i for i in reversed(range(fronts.bit_length() - 1))]
    orders = [bits, bits[1::-1] + bits[2:]]
    got, rels = [], []
    for part, order, z0 in zip(parts, orders, (0, 2)):
        part, fs = part[None], [0]
        for bit in order[:-1]:
            part = jnp.concatenate([part, swap(part, "front", bit)], 0)
            fs = fs + [f ^ bit for f in fs]
        got += [part, swap(part, "front", order[-1])]
        rels += [(fs, z0), ([f ^ order[-1] for f in fs], z0)]
    return got, rels


def shards(
    child_diag, child_top, child_rows, row_owner, row_slot, col_block, parent_diag, parent_rows
):
    fronts = lax.axis_size("front")
    z, f = lax.axis_index("blk"), lax.axis_index("front")
    plan = lax.dynamic_slice_in_dim(jnp.array(PLAN, jnp.int32), z, 1, 0)[0]
    info = jnp.concatenate([plan, jnp.stack([z, f]).astype(jnp.int32)])
    strip_rows = T // fronts
    base = lax.dynamic_slice_in_dim(parent_diag.reshape(2, T, 4 * Q), f * strip_rows, strip_rows, 1)
    barrier = lax.optimization_barrier

    up, down = call(pieces_kernel, "pieces", (sds(3, Q, Q),) * 2, (info, child_diag), 1)
    ua1, da1 = lax.ppermute(up, "blk", UP), lax.ppermute(down, "blk", DOWN)
    tu1, td1 = lax.ppermute(child_top, "blk", UP), lax.ppermute(child_top, "blk", DOWN)
    l0, u0 = call(own_stage, "child_panel", (sds(Q, Q), sds(Q, 3 * Q)), (info, child_diag), 1, [vmem(Q, 4 * Q)])
    solved = rows_stage(0, info, child_rows, (), (), l0)
    ua1, da1, l0, solved, base = barrier((ua1, da1, l0, solved, base))

    ua2, da2 = lax.ppermute(ua1[:2], "blk", UP[1:]), lax.ppermute(da1[:2], "blk", DOWN[:2])
    up_pick, down_pick = tuple((0, i) for i in range(3)), tuple((1, i) for i in range(3))
    l1, u1 = child_stage(1, info, (ua1, da1), (u0,), (down_pick, up_pick, down_pick, up_pick))
    solved1 = rows_stage(1, info, child_rows, (solved,), (u0,), l1)
    ua2, da2, tu1, td1, l1, solved1 = barrier((ua2, da2, tu1, td1, l1, solved1))

    u3, d3 = lax.ppermute(ua2[0], "blk", UP[2:]), lax.ppermute(da2[0], "blk", DOWN[:1])
    tu2, td2 = lax.ppermute(tu1, "blk", UP[1:]), lax.ppermute(td1, "blk", DOWN[:2])
    l2, u2 = child_stage(2, info, (da2, da1, ua1, ua2), (u0, u1), tuple(((i, 0), (i, 1)) for i in range(4)))
    solved2 = rows_stage(2, info, child_rows, (solved, solved1), (u0, u1), l2)
    u3, d3, tu2, td2, l2, solved2 = barrier((u3, d3, tu2, td2, l2, solved2))

    tu3, td3 = lax.ppermute(tu2, "blk", UP[2:]), lax.ppermute(td2, "blk", DOWN[:1])
    (l3,) = child_stage(3, info, (d3, da2, ua2, u3), (u0, u1, u2),
                        (((0, None),), ((1, 0),), ((2, 0),), ((3, None),)))
    tu3, td3, l3 = barrier((tu3, td3, l3))
    factor = (u0, u1, u2, l0, l1, l2, l3)
    top_solved, cross = call(
        top_kernel, "top_solved", (sds(4 * T, 4 * Q), sds(fronts, 9, strip_rows, T)),
        (info, col_block, td1, td2, td3, tu1, tu2, tu3, child_top, *factor), 2, [vmem(4 * T, 4 * Q)], 6)

    strips = lax.all_to_all(cross, "front", 0, 0, tiled=True)
    solved3 = rows_stage(3, info, child_rows, (solved, solved1, solved2), (u0, u1, u2), l3)
    strips, solved3, top_solved = barrier((strips, solved3, top_solved))
    strip = call(strip_kernel, "diag_strip", sds(9, strip_rows, T), (info, strips, base), 1, (), 1)
    near = [swap(strip, "blk", bit) for bit in (1, 2, 3)]
    schur = call(schur_kernel, "schur", sds(4, child_rows.shape[0], T),
                 (solved, solved1, solved2, solved3, top_solved), 0)
    *near, schur = barrier((*near, schur))
    if strip_rows % 8 == 0:
        got, rels = everywhere((jnp.stack([strip, near[0]]), jnp.stack(near[1:])))
    else:
        whole = lax.all_gather(strip, ("front", "blk"), axis=0).reshape(fronts, 4, 9, strip_rows, T)
        got, rels = [whole.transpose(1, 2, 0, 3, 4).reshape(4, 9, T, T)], []

    arrived = lax.all_to_all(schur, "blk", 0, 0, tiled=True)
    p0, k0, rest, v0 = call(
        parent_first(rels), "parent_first", (sds(Q, Q), sds(Q, Q), sds(3 * Q, 3 * Q), sds(Q, 3 * Q)),
        (info, *got), 1, [vmem(Q, 4 * Q), vmem(4, 9, T, T)], len(got))
    arrived, p0, k0, rest, v0 = barrier((arrived, p0, k0, rest, v0))
    outgoing = call(pack_kernel, "outgoing", sds(fronts, 4 * T + 8, T),
                    (info, col_block, row_owner[0, :, 0], row_slot[0], arrived.reshape(-1, T, T)), 4, (), 1)
    received = lax.all_to_all(outgoing, "front", 0, 0, tiled=True)
    p1, k1, v1 = call(parent_next(1), "parent_next", (sds(Q, Q), sds(Q, Q), sds(Q, 2 * Q)),
                      (rest, v0), 0, [vmem(Q, 3 * Q)])
    p2, k2, v2 = call(parent_next(2), "parent_next", (sds(Q, Q), sds(Q, Q), sds(Q, Q)),
                      (rest, v0, v1), 0, [vmem(Q, 2 * Q)])
    received, p2, k2, v2 = barrier((received, p2, k2, v2))
    updated = call(land_kernel, "updated", sds(4, T, Q), (received, parent_rows), 0, (), 1)
    row_major = lax.all_to_all(updated, "blk", 0, 0, tiled=True)
    p3, own_rows = call(parent_last, "parent_last", (sds(Q, Q), sds(Q, 4 * Q)),
                        (info, rest, v0, v1, v2, k0, k1, k2), 1, [vmem(Q, Q), vmem(Q, Q)])
    panel = call(panel_kernel, "parent_panel", sds(T, 4 * Q), (row_major, v0, v1, v2, p0, p1, p2, p3), 0, (), 1)
    return own_rows, panel


def solution(mesh):
    return jax.shard_map(
        shards,
        mesh=mesh,
        in_specs=(
            P(("front", "blk"), None),
            P(("front", "blk"), None),
            P(("front", "blk"), None),
            P("front", None, None),
            P("front", None),
            P("front", None),
            P("blk", None),
            P("front", "blk"),
        ),
        out_specs=(P("blk", None), P(("front", "blk"), None)),
        check_vma=False,
    )
```

```python
import math

import jax
import jax.numpy as jnp
from jax import lax
from jax.experimental import pallas as pl
from jax.experimental.pallas import tpu as pltpu
from jax.sharding import PartitionSpec as P

HIGHEST = lax.Precision.HIGHEST
T = 128
S = 32
G = 16
Q = 256

PLAN = (
    (0, 1, 2, 3, 0, 2, 3, 0, 0, 0),
    (1, 0, 2, 3, 1, 0, 0, 1, 2, 3),
    (2, 3, 1, 0, 2, 1, 0, 2, 3, 3),
    (3, 2, 1, 0, 0, 0, 0, 3, 1, 0),
)
UP = ((0, 1), (1, 2), (2, 3))
DOWN = ((1, 0), (2, 1), (3, 2))
F32 = jnp.float32


def mm(x, y, a, b):
    return lax.dot_general(x, y, (((a,), (b,)), ((), ())), precision=HIGHEST, preferred_element_type=F32)


def mm_nn(x, y):
    return mm(x, y, 1, 0)


def mm_nt(x, y):
    return mm(x, y, 1, 1)


def mm_tn(x, y):
    return mm(x, y, 0, 0)


def call(body, name, out_shape, args, smem, scratch=(), loose=0, blocks=()):
    vm = pl.BlockSpec(memory_space=pltpu.VMEM)
    outs = out_shape if isinstance(out_shape, tuple) else (out_shape,)
    held = [*outs, *args, *[jax.ShapeDtypeStruct(x.shape, x.dtype) for x in scratch]]
    size = sum(4 * math.prod(x.shape) for x in held)
    fixed = smem + loose
    args = [*args[:fixed], *[pltpu.with_memory_space_constraint(x, pltpu.HBM) for x in args[fixed:]]]
    specs = [vm] * (len(args) - smem)
    for at, shape, pick in blocks:
        specs[at - smem] = pl.BlockSpec(shape, lambda i, info, *_, pick=pick: (0, info[pick]))
    got = pl.pallas_call(
        body,
        grid_spec=pltpu.PrefetchScalarGridSpec(
            num_scalar_prefetch=smem, grid=(1,), in_specs=specs, out_specs=[vm] * len(outs),
            scratch_shapes=list(scratch)),
        out_shape=[pltpu.HBM(x.shape, x.dtype) for x in outs],
        compiler_params=pltpu.CompilerParams(vmem_limit_bytes=2 * size + 8 * 1024 * 1024),
        name=name,
    )(*args)
    return tuple(got) if isinstance(out_shape, tuple) else got[0]


def sds(*shape):
    return jax.ShapeDtypeStruct(shape, F32)


def eliminate32(rows, inv_rows, lane0):
    ng = S // 8
    sub = lax.broadcasted_iota(jnp.int32, (8, T), 0)
    xa = [rows[8 * g:8 * g + 8] for g in range(ng)]
    xi = [inv_rows[8 * g:8 * g + 8] for g in range(ng)]
    def row(groups, i):
        return jnp.broadcast_to(groups[i // 8][i % 8:i % 8 + 1], (8, T))

    scale = [jnp.zeros((8, T), F32) for _ in range(ng)]
    bc = {}
    for j in range(0, S, 2):
        gj, rj = j // 8, j % 8
        end = j // G * G + G
        if j % G == 0:
            for c in range(j, end):
                bc[c] = [None] * (c // 8) + [
                    jnp.broadcast_to(xa[g][:, lane0 + c:lane0 + c + 1], (8, T)) for g in range(c // 8, ng)]
            p11, p21, p22 = row(bc[j], j), row(bc[j], j + 1), row(bc[j + 1], j + 1)
        c1, c2 = bc[j], bc[j + 1]
        det = p11 * p22 - p21 * p21
        rd = pl.reciprocal(det, approx=True)
        m1 = {c: row(c1, c) for c in range(j + 2, end)}
        m2 = {c: row(c2, c) for c in range(j + 2, end)}
        if j + 2 < end:
            a, b = j + 2, j + 3
            w1a, w2a = m1[a] * p22 - m2[a] * p21, m2[a] * p11 - m1[a] * p21
            w1b, w2b = m1[b] * p22 - m2[b] * p21, m2[b] * p11 - m1[b] * p21
            n11 = row(bc[a], a) - (w1a * m1[a] + w2a * m2[a]) * rd
            n21 = row(bc[a], b) - (w1b * m1[a] + w2b * m2[a]) * rd
            n22 = row(bc[b], b) - (w1b * m1[b] + w2b * m2[b]) * rd
        t1 = [None if g < gj else (c1[g] * p22 - c2[g] * p21) * rd for g in range(ng)]
        t2 = [None if g < gj else (c2[g] * p11 - c1[g] * p21) * rd for g in range(ng)]
        for c in range(j + 2, end):
            for g in range(c // 8, ng):
                bc[c][g] = bc[c][g] - (t1[g] * m1[c] + t2[g] * m2[c])
        r1 = lax.rsqrt(p11)
        q1 = r1 * r1
        r2 = lax.rsqrt(det * q1)
        scale[gj] = jnp.where(sub == rj, r1, jnp.where(sub == rj + 1, r2, scale[gj]))
        k1, k2 = list(t1), list(t2)
        k1[gj] = jnp.where(sub > rj + 1, t1[gj], jnp.where(sub == rj + 1, p21 * q1, 0.0))
        k2[gj] = jnp.where(sub > rj + 1, t2[gj], 0.0)
        for x in (xa, xi):
            x1, x2 = row(x, j), row(x, j + 1)
            for g in range(gj, ng):
                x[g] = x[g] - (k1[g] * x1 + k2[g] * x2)
        if j + 2 < end:
            p11, p21, p22 = n11, n21, n22
    return (
        jnp.concatenate([a * s for a, s in zip(xa, scale)], 0),
        jnp.concatenate([a * s for a, s in zip(xi, scale)], 0),
    )


def split3(x):
    h = x.astype(jnp.bfloat16)
    r = x - h.astype(F32)
    m = r.astype(jnp.bfloat16)
    return h, m, (r - m.astype(F32)).astype(jnp.bfloat16)


def factor128(a):
    r = lax.broadcasted_iota(jnp.int32, (T, T), 0)
    c = lax.broadcasted_iota(jnp.int32, (T, T), 1)
    diag = jnp.where(r == c, a, 0.0)
    across = jnp.sum(diag, axis=0, keepdims=True)
    s_row, s_col = lax.rsqrt(across), lax.rsqrt(jnp.sum(diag, axis=1, keepdims=True))
    a = a * s_row * s_col
    inv = jnp.where(r == c, 1.0, 0.0).astype(F32)
    us, ls = [], []
    for s in range(T // S):
        u, li = eliminate32(a[:S], inv[:S], s * S)
        us.append(u)
        ls.append(li)
        if s < T // S - 1:
            h, m, l = split3(u)
            hi, mi, lo = split3(li)
            left = jnp.concatenate([h, h, m, h, l, m], 0)
            right = jnp.concatenate([jnp.concatenate([x, y], 1) for x, y in
                                     ((h, hi), (m, mi), (h, hi), (l, lo), (h, hi), (m, mi))], 0)
            both = lax.dot_general(left, right, (((0,), (0,)), ((), ())), preferred_element_type=F32)
            a = a[S:] - both[(s + 1) * S:, :T]
            inv = inv[S:] - both[(s + 1) * S:, T:]
    u = jnp.concatenate(us, 0) * (across * s_row)
    return jnp.where(c >= r, u, 0.0), jnp.concatenate(ls, 0) * s_row


def factor_panel(pan, li_ref, keep=None, beside=None):
    def half(i, carry):
        d = pl.ds(pl.multiple_of(i * T, T), T)
        a = pan[d, d]
        if beside is not None:
            beside(i)
        u, li = factor128(a)
        li_ref[d, d] = li
        if keep is not None:
            keep[d, d] = u
        @pl.when(i == 0)
        def _():
            u12 = mm_nn(li, pan[:T, T:])
            pan[:T, T:] = u12
            pan[T:, T:] -= mm_tn(u12, u12)
            if keep is not None:
                keep[:T, T:] = u12
                keep[T:, :T] = jnp.zeros((T, T), F32)
        return carry
    lax.fori_loop(0, 2, half, 0)
    li_ref[:T, T:] = jnp.zeros((T, T), F32)
    li_ref[T:, :T] = -mm_nn(li_ref[T:, T:], mm_tn(pan[:T, T:], li_ref[:T, :T]))


def update_near(pan, p, us):
    for q in range(p):
        o = (p - q - 1) * Q
        pan[...] -= mm_tn(us[q][:, o:o + Q], us[q][:, o:o + Q])


def update_far(far, p, us, i):
    at = pl.ds(pl.multiple_of(i * T, T), T)
    for q in range(p):
        o = (p - q - 1) * Q
        far[at, :] -= mm_tn(us[q][:, pl.ds(pl.multiple_of(o + i * T, T), T)], us[q][:, o + Q:])


def child_kernel(p, picks, count):
    def body(info, *refs):
        got, (r_ref, t_ref), rest = refs[:count], refs[count:count + 2], refs[count + 2:]
        last = p == 3
        if last:
            (d1, p1, d2, p2), lis, rest = rest[:4], rest[4:7], rest[7:]
        us, before, rest = rest[:p], rest[p:2 * p], rest[2 * p:]
        li_ref, solved, u_ref, pan, x, far = rest
        if p == 0:
            pan[...] = got[0][:, pl.ds(pl.multiple_of(info[0] * Q, Q), Q)]
            for i in range(3):
                far[:, i * Q:(i + 1) * Q] = got[0][:, pl.ds(pl.multiple_of(info[i + 1] * Q, Q), Q)]
        for z in range(4 if p else 0):
            @pl.when(info[10] == z)
            def _():
                for i, (a, lead) in enumerate(picks[z]):
                    value = got[a][...] if lead is None else got[a][lead]
                    if i == 0:
                        pan[...] = value
                    else:
                        far[:, (i - 1) * Q:i * Q] = value
        m = r_ref.shape[0]
        x[:m] = r_ref[...]
        x[m:] = t_ref[...]
        if last:
            near, tops = u_ref, far
            tops[:T] = d1[...]
            tops[T:2 * T] = p1[...]
            for ref, here in ((d2, info[10] < 2), (p2, info[10] >= 2)):
                @pl.when(here)
                def _():
                    tops[2 * T:] = ref[...]
        update_near(pan, p, us)
        def beside(i):
            if p < 3:
                update_far(far, p, us, i)
            n = x.shape[0] // 2
            at = pl.ds(pl.multiple_of(i * n, n), n)
            for q in range(p):
                o = (p - q - 1) * Q
                x[at, :] -= mm_nn(before[q][at, :], us[q][:, o:o + Q])
            if last:
                n = tops.shape[0] // 2
                at = pl.ds(pl.multiple_of(i * n, n), n)
                for k in range(4):
                    y = tops[at, pl.ds(pl.multiple_of(info[k] * Q, Q), Q)]
                    for q in range(k):
                        o = (k - q - 1) * Q
                        y = y - mm_nn(near[at, q * Q:(q + 1) * Q], us[q][:, o:o + Q])
                    near[at, k * Q:(k + 1) * Q] = mm_nt(y, lis[k][...]) if k < 3 else y
        factor_panel(pan, li_ref, None, beside if p else None)
        if p < 3:
            u_ref[...] = mm_nn(li_ref[...], far[...])
        solved[...] = mm_nt(x[...], li_ref[...])
        if last:
            near[:, 3 * Q:] = mm_nt(near[:, 3 * Q:], li_ref[...])
    return body


def child_stage(p, info, got, rows, top, us, before, picks=(), tops=(), lis=()):
    w, n = max(1, 3 - p) * Q, rows.shape[0] + top.shape[0]
    out = (sds(Q, Q), sds(n, Q), sds(Q, w) if p < 3 else sds(3 * T, 4 * Q))
    k = 1 + len(got)
    return call(
        child_kernel(p, picks, len(got)), "child_panel", out, (info, *got, rows, top, *tops, *lis, *us, *before), 1,
        [vmem(Q, Q), vmem(n, Q), vmem(Q, w) if p < 3 else vmem(3 * T, 4 * Q)], len(got) if p else 0,
        ((k, (rows.shape[0], Q), p), (k + 1, (top.shape[0], Q), p)))


def solve_rows(read, us, lis, out):
    for p in range(4):
        x = read(p)
        for q in range(p):
            o = (p - q - 1) * Q
            x = x - mm_nn(out[:, q * Q:(q + 1) * Q], us[q][:, o:o + Q])
        out[:, p * Q:(p + 1) * Q] = mm_nt(x, lis[p][...])


def pieces_kernel(info, c_ref, up, down):
    for i in range(3):
        up[i] = c_ref[:, pl.ds(pl.multiple_of(info[4 + i] * Q, Q), Q)]
        down[i] = c_ref[:, pl.ds(pl.multiple_of(info[7 + i] * Q, Q), Q)]


def top_kernel(info, cb, d3, p3, near, s0, s1, s2, s3, u0, u1, u2, l0, l1, l2, l3, out, cross, full, done):
    z = info[10]
    m = s0.shape[0] - T
    def at(k):
        return pl.ds(pl.multiple_of(k * T, T), T)
    for ref, end in ((d3, 0), (p3, 3)):
        @pl.when(z == end)
        def _():
            full[...] = ref[...]
    @pl.when((z == 0) | (z == 3))
    def _():
        solve_rows(lambda p: full[:, pl.ds(pl.multiple_of(info[p] * Q, Q), Q)], (u0, u1, u2), (l0, l1, l2, l3), done)
        out[at(3 - z), :] = done[...]
    for shift, here, i in ((1, z < 3, 0), (-1, z > 0, 1), (2, z < 2, 2), (-2, z >= 2, 2)):
        @pl.when(here)
        def _():
            out[at(z + shift), :] = near[i * T:(i + 1) * T, :]
    here = pl.ds(pl.multiple_of(z * T, T), T)
    for p, s in enumerate((s0, s1, s2, s3)):
        out[here, p * Q:(p + 1) * Q] = s[m:, :]
    rows = (cross.shape[1] - 8) // 3
    for d in range(3):
        k = lax.rem(z + d, 4)
        block = mm_nt(out[here, :], out[pl.ds(pl.multiple_of(k * T, T), T), :])
        for r in range(cross.shape[0]):
            cross[r, d * rows:(d + 1) * rows, :] = block[r * rows:(r + 1) * rows]
    which = lax.broadcasted_iota(jnp.int32, (8, T), 0)
    flags = jnp.zeros((8, T), F32)
    for k in range(4):
        flags = jnp.where(which == k, cb[0, k].astype(F32), flags)
    for r in range(cross.shape[0]):
        cross[r, 3 * rows:, :] = flags


def schur_kernel(r0, r1, r2, r3, t_ref, *refs):
    out = refs[-1]
    for k in range(4):
        at = slice(k * T, (k + 1) * T)
        out[k] = sum(mm_nt(r[...], t_ref[at, p * Q:(p + 1) * Q]) for p, r in enumerate((r0, r1, r2, r3)))


def schur_half(solved, top_solved, rows, half, into=()):
    n = rows // 2
    fixed = [pltpu.with_memory_space_constraint(x, pltpu.HBM) for x in (*solved, top_solved, *into)]
    return pl.pallas_call(
        schur_kernel,
        grid=(1,),
        in_specs=[pl.BlockSpec((n, Q), lambda i: (half, 0))] * 4 + [pl.BlockSpec(memory_space=pltpu.VMEM)]
        + [pl.BlockSpec(memory_space=pl.ANY)] * len(into),
        out_specs=pl.BlockSpec((4, n, T), lambda i: (0, half, 0)),
        out_shape=pltpu.HBM((4, rows, T), F32),
        input_output_aliases={5: 0} if into else {},
        compiler_params=pltpu.CompilerParams(vmem_limit_bytes=24 * 1024 * 1024),
        name="schur",
    )(*fixed)


def strip_kernel(info, recv, base, out):
    z = info[10]
    n1, n2 = lax.rem(z + 1, 4), lax.rem(z + 2, 4)
    def start(a, k, b):
        return base[a, :, pl.ds(pl.multiple_of(k * Q + b * T, T), T)]
    out[0] = start(0, z, 0)
    out[1] = start(0, z, 1)
    out[2] = start(1, z, 1)
    for a in range(2):
        for b in range(2):
            out[3 + 2 * a + b] = start(a, n1, b)
    low = z < 2
    @pl.when(low)
    def _():
        out[7] = start(0, n2, 0)
        out[8] = start(1, n2, 0)
    @pl.when(jnp.logical_not(low))
    def _():
        out[7] = start(1, n2, 0)
        out[8] = start(1, n2, 1)
    rows = out.shape[1]
    sums = [jnp.zeros((rows, T), F32)] * 9
    first = jnp.where(low, 1.0, 0.0).astype(F32)
    for f in range(recv.shape[0]):
        def flag(k):
            return jnp.broadcast_to(recv[f, pl.ds(3 * rows + k, 1), :], (rows, T))
        a0, a1, a2 = flag(z), flag(n1), flag(n2)
        x0, x1, x2 = (recv[f, d * rows:(d + 1) * rows, :] for d in range(3))
        half = first * a0 + (1.0 - first) * a2
        kept = first * (1.0 - a2) + (1.0 - first) * a0
        places = [(0, x0, 1.0 - a0), (2, x0, a0)]
        for a in range(2):
            for b in range(2):
                places.append((3 + 2 * a + b, x1, (a0 if a else 1.0 - a0) * (a1 if b else 1.0 - a1)))
        places += [(7, x2, kept * (1.0 - half)), (8, x2, kept * half)]
        for i, x, here in places:
            sums[i] = sums[i] + jnp.where(here > 0.5, x, 0.0)
    for i in (0, 2, 3, 4, 5, 6, 7, 8):
        out[i] = out[i] - sums[i]


def nine(z):
    b, n1, n2 = 2 * z, 2 * ((z + 1) % 4), 2 * ((z + 2) % 4)
    places = [(b, b), (b, b + 1), (b + 1, b + 1)]
    places += [(b + i, n1 + j) for i in range(2) for j in range(2)]
    places += [(b, n2), (b + 1, n2)] if z < 2 else [(b + 1, n2), (b + 1, n2 + 1)]
    return [(i, j, False) if i <= j else (j, i, True) for i, j in places]


def parent_first(rels):
    def body(info, *refs):
        got = refs[:max(1, len(rels))]
        l0, keep, r1, r2, r3, u0, pan, far, tiles = refs[len(got):]
        z, f = info[10], info[11]
        if rels:
            for ref, (fs, z0) in zip(got, rels):
                rows = ref.shape[3]
                for i, rf in enumerate(fs):
                    src = jnp.bitwise_xor(f, rf)
                    for j in range(ref.shape[1]):
                        zz = jnp.bitwise_xor(z, z0 + j)
                        tiles[zz, :, pl.ds(pl.multiple_of(src * rows, rows), rows), :] = ref[i, j]
        else:
            tiles[...] = got[0][...]
        near = (pan, r1, r2, r3)
        for zz in range(4):
            for i, (r, c, turned) in enumerate(nine(zz)):
                block = tiles[zz, i]
                target, r, c = near[r // 2], r % 2, c - r // 2 * 2
                if target is pan and c >= 2:
                    target, c = far, c - 2
                target[r * T:(r + 1) * T, c * T:(c + 1) * T] = block.T if turned else block
        for target in near:
            target[T:, :T] = jnp.zeros((T, T), F32)
        factor_panel(pan, l0, keep)
        u0[...] = mm_nn(l0[...], far[...])
    return body


def parent_middle(r1, r2, u0, l1, l2, k1, k2, u1, u2, pan, far):
    us = (u0, u1)
    for p, src, li, keep, u in ((1, r1, l1, k1, u1), (2, r2, l2, k2, u2)):
        pan[...] = src[:, :Q]
        wide = far.at[:, :(3 - p) * Q]
        wide[...] = src[:, Q:]
        update_near(pan, p, us)
        factor_panel(pan, li, keep, lambda i: update_far(wide, p, us, i))
        u[...] = mm_nn(li[...], wide[...])


def own_kernel(info, u0, u1, u2, k0, k1, k2, own):
    us, keeps = (u0, u1, u2), (k0, k1, k2)
    for zz in range(4):
        @pl.when(info[10] == zz)
        def _():
            for q in range(4):
                if q < zz:
                    block = us[q][:, (zz - q - 1) * Q:(zz - q) * Q].T
                elif q == zz and zz < 3:
                    block = keeps[zz][...].T
                else:
                    block = jnp.zeros((Q, Q), F32)
                own[:, q * Q:(q + 1) * Q] = block


def last_kernel(info, r3, u0, u1, u2, _, li, corner, pan, keep):
    pan[...] = r3[...]
    update_near(pan, 3, (u0, u1, u2))
    factor_panel(pan, li, keep)
    @pl.when(info[10] == 3)
    def _():
        corner[...] = keep[...].T
    @pl.when(info[10] < 3)
    def _():
        corner[...] = jnp.zeros((Q, Q), F32)


def parent_last(info, r3, us, own):
    vm = pl.BlockSpec(memory_space=pltpu.VMEM)
    fixed = [pltpu.with_memory_space_constraint(x, pltpu.HBM) for x in (r3, *us, own)]
    return pl.pallas_call(
        last_kernel,
        grid_spec=pltpu.PrefetchScalarGridSpec(
            num_scalar_prefetch=1, grid=(1,), in_specs=[vm] * 4 + [pl.BlockSpec(memory_space=pl.ANY)],
            out_specs=[vm, pl.BlockSpec((Q, Q), lambda i, info: (0, 3))], scratch_shapes=[vmem(Q, Q), vmem(Q, Q)]),
        out_shape=[pltpu.HBM((Q, Q), F32), pltpu.HBM(own.shape, F32)],
        input_output_aliases={5: 1},
        compiler_params=pltpu.CompilerParams(vmem_limit_bytes=24 * 1024 * 1024),
        name="parent_last",
    )(info, *fixed)


def vmem(*shape):
    return pltpu.VMEM(shape, F32)


def panel_kernel(x_ref, u0, u1, u2, l0, l1, l2, l3, out):
    solve_rows(lambda p: x_ref[p], (u0, u1, u2), (l0, l1, l2, l3), out)


def pack_kernel(info, cb, owner, slot, x_ref, out):
    out[...] = jnp.zeros(out.shape, F32)
    def one(b, carry):
        o, at = owner[b], pl.ds(pl.multiple_of(slot[b] * T, T), T)
        out[o, at, :] = out[o, at, :] + x_ref[b]
        return carry
    lax.fori_loop(0, x_ref.shape[0], one, 0)
    out[:, 4 * T:, :] = jnp.full((out.shape[0], 8, T), cb[0, info[10]].astype(F32))


def land_kernel(recv, rows_ref, out):
    for s in range(4):
        at = slice(s * T, (s + 1) * T)
        def one(f, carry):
            right = jnp.broadcast_to(recv[f, 4 * T:4 * T + 1, :], (T, T)) > 0.5
            x = recv[f, at, :]
            return carry[0] - jnp.where(right, 0.0, x), carry[1] - jnp.where(right, x, 0.0)
        out[s, :, :T], out[s, :, T:] = lax.fori_loop(0, recv.shape[0], one, (rows_ref[at, :T], rows_ref[at, T:]))


def swap(x, axis, bit):
    n = lax.axis_size(axis)
    return lax.ppermute(x, axis, [(i, i ^ bit) for i in range(n)])


def everywhere(parts):
    fronts = lax.axis_size("front")
    bits = [1 << i for i in reversed(range(fronts.bit_length() - 1))]
    orders = [bits, bits[1::-1] + bits[2:]]
    got, rels = [], []
    for part, order, z0 in zip(parts, orders, (0, 2)):
        part, fs = part[None], [0]
        for bit in order[:-1]:
            part = jnp.concatenate([part, swap(part, "front", bit)], 0)
            fs = fs + [f ^ bit for f in fs]
        got += [part, swap(part, "front", order[-1])]
        rels += [(fs, z0), ([f ^ order[-1] for f in fs], z0)]
    return got, rels


def shards(
    child_diag, child_top, child_rows, row_owner, row_slot, col_block, parent_diag, parent_rows
):
    fronts = lax.axis_size("front")
    z, f = lax.axis_index("blk"), lax.axis_index("front")
    plan = lax.dynamic_slice_in_dim(jnp.array(PLAN, jnp.int32), z, 1, 0)[0]
    info = jnp.concatenate([plan, jnp.stack([z, f]).astype(jnp.int32)])
    strip_rows = T // fronts
    base = lax.dynamic_slice_in_dim(parent_diag.reshape(2, T, 4 * Q), f * strip_rows, strip_rows, 1)
    barrier = lax.optimization_barrier

    up, down = call(pieces_kernel, "pieces", (sds(3, Q, Q),) * 2, (info, child_diag), 1)
    ua1, da1 = lax.ppermute(up, "blk", UP), lax.ppermute(down, "blk", DOWN)
    l0, s0, u0 = child_stage(0, info, (child_diag,), child_rows, child_top, (), ())
    sent, l0 = barrier((child_top, l0))
    tu1, td1 = lax.ppermute(sent, "blk", UP), lax.ppermute(sent, "blk", DOWN)
    ua1, da1, l0, base = barrier((ua1, da1, l0, base))

    ua2, da2 = lax.ppermute(ua1[:2], "blk", UP[1:]), lax.ppermute(da1[:2], "blk", DOWN[:2])
    up_pick, down_pick = tuple((0, i) for i in range(3)), tuple((1, i) for i in range(3))
    l1, s1, u1 = child_stage(1, info, (ua1, da1), child_rows, child_top, (u0,), (s0,),
                             (down_pick, up_pick, down_pick, up_pick))
    ua2, da2, tu1, td1, l1 = barrier((ua2, da2, tu1, td1, l1))

    u3, d3 = lax.ppermute(ua2[0], "blk", UP[2:]), lax.ppermute(da2[0], "blk", DOWN[:1])
    tu2, td2 = lax.ppermute(tu1, "blk", UP[1:]), lax.ppermute(td1, "blk", DOWN[:2])
    l2, s2, u2 = child_stage(2, info, (da2, da1, ua1, ua2), child_rows, child_top, (u0, u1), (s0, s1),
                             tuple(((i, 0), (i, 1)) for i in range(4)))
    u3, d3, tu2, td2, l2 = barrier((u3, d3, tu2, td2, l2))

    tu3, td3 = lax.ppermute(tu2, "blk", UP[2:]), lax.ppermute(td2, "blk", DOWN[:1])
    l3, s3, near = child_stage(3, info, (d3, da2, ua2, u3), child_rows, child_top, (u0, u1, u2), (s0, s1, s2),
                               (((0, None),), ((1, 0),), ((2, 0),), ((3, None),)), (td1, tu1, td2, tu2), (l0, l1, l2))
    tu3, td3, l3 = barrier((tu3, td3, l3))
    top_solved, cross = call(
        top_kernel, "top_solved", (sds(4 * T, 4 * Q), sds(fronts, 3 * strip_rows + 8, T)),
        (info, col_block, td3, tu3, near, s0, s1, s2, s3, u0, u1, u2, l0, l1, l2, l3), 2,
        [vmem(T, 4 * Q)] * 2, 2)

    strips = lax.all_to_all(cross, "front", 0, 0, tiled=True)
    solved, rows = (s0, s1, s2, s3), child_rows.shape[0]
    schur = schur_half(solved, top_solved, rows, 0)
    strips, schur = barrier((strips, schur))
    strip = call(strip_kernel, "diag_strip", sds(9, strip_rows, T), (info, strips, base), 1, (), 1)
    line = [swap(strip, "blk", bit) for bit in (1, 2, 3)]
    schur = schur_half(solved, top_solved, rows, 1, (schur,))
    *line, schur = barrier((*line, schur))
    if strip_rows % 8 == 0:
        got, rels = everywhere((jnp.stack([strip, line[0]]), jnp.stack(line[1:])))
    else:
        whole = lax.all_gather(strip, ("front", "blk"), axis=0).reshape(fronts, 4, 9, strip_rows, T)
        got, rels = [whole.transpose(1, 2, 0, 3, 4).reshape(4, 9, T, T)], []

    arrived = lax.all_to_all(schur, "blk", 0, 0, tiled=True)
    p0, k0, r1, r2, r3, v0 = call(
        parent_first(rels), "parent_first",
        (sds(Q, Q), sds(Q, Q), sds(Q, 3 * Q), sds(Q, 2 * Q), sds(Q, Q), sds(Q, 3 * Q)),
        (info, *got), 1, [vmem(Q, Q), vmem(Q, 3 * Q), vmem(4, 9, T, T)], len(got))
    arrived, p0, k0, r1, r2, r3, v0 = barrier((arrived, p0, k0, r1, r2, r3, v0))
    outgoing = call(pack_kernel, "outgoing", sds(fronts, 4 * T + 8, T),
                    (info, col_block, row_owner[0, :, 0], row_slot[0], arrived.reshape(-1, T, T)), 4, (), 1)
    received = lax.all_to_all(outgoing, "front", 0, 0, tiled=True)
    p1, p2, k1, k2, v1, v2 = call(
        parent_middle, "parent_middle",
        (sds(Q, Q), sds(Q, Q), sds(Q, Q), sds(Q, Q), sds(Q, 2 * Q), sds(Q, Q)), (r1, r2, v0), 0,
        [vmem(Q, Q), vmem(Q, 2 * Q)])
    own_rows = call(own_kernel, "own_rows", sds(Q, 4 * Q), (info, v0, v1, v2, k0, k1, k2), 1)
    received, p2, v2, own_rows = barrier((received, p2, v2, own_rows))
    updated = call(land_kernel, "updated", sds(4, T, Q), (received, parent_rows), 0, (), 1)
    row_major = lax.all_to_all(updated, "blk", 0, 0, tiled=True)
    p3, own_rows = parent_last(info, r3, (v0, v1, v2), own_rows)
    panel = call(panel_kernel, "parent_panel", sds(T, 4 * Q), (row_major, v0, v1, v2, p0, p1, p2, p3), 0, (), 1)
    return own_rows, panel


def solution(mesh):
    return jax.shard_map(
        shards,
        mesh=mesh,
        in_specs=(
            P(("front", "blk"), None),
            P(("front", "blk"), None),
            P(("front", "blk"), None),
            P("front", None, None),
            P("front", None),
            P("front", None),
            P("blk", None),
            P("front", "blk"),
        ),
        out_specs=(P("blk", None), P(("front", "blk"), None)),
        check_vma=False,
    )
```

```python
import math

import jax
import jax.numpy as jnp
from jax import lax
from jax.experimental import pallas as pl
from jax.experimental.pallas import tpu as pltpu
from jax.sharding import PartitionSpec as P

T = 128
S = 32
G = 16
Q = 256

PLAN = (
    (0, 1, 2, 3, 0, 2, 3, 0, 0, 0),
    (1, 0, 2, 3, 1, 0, 0, 1, 2, 3),
    (2, 3, 1, 0, 2, 1, 0, 2, 3, 3),
    (3, 2, 1, 0, 0, 0, 0, 3, 1, 0),
)
UP = ((0, 1), (1, 2), (2, 3))
DOWN = ((1, 0), (2, 1), (3, 2))
F32 = jnp.float32


def pieces_of(x, count):
    got = []
    for _ in range(count):
        got.append(x.astype(jnp.bfloat16))
        x = x - got[-1].astype(F32)
    return got


def mm(x, y, a, b, left, right):
    xs, ys = pieces_of(x, max(left) + 1), pieces_of(y, max(right) + 1)
    return lax.dot_general(
        jnp.concatenate([xs[i] for i in left], a), jnp.concatenate([ys[i] for i in right], b),
        (((a,), (b,)), ((), ())), preferred_element_type=F32)


SIX = ((0, 0, 1, 0, 2, 1), (0, 1, 0, 2, 0, 1))
THREE = ((0, 0, 1), (0, 1, 0))


def mm_nn(x, y, terms=SIX):
    return mm(x, y, 1, 0, *terms)


def mm_nt(x, y, terms=SIX):
    return mm(x, y, 1, 1, *terms)


def mm_tn(x, y, terms=SIX):
    return mm(x, y, 0, 0, *terms)


def call(body, name, out_shape, args, smem, scratch=(), loose=0, blocks=()):
    vm = pl.BlockSpec(memory_space=pltpu.VMEM)
    outs = out_shape if isinstance(out_shape, tuple) else (out_shape,)
    held = [*outs, *args, *[jax.ShapeDtypeStruct(x.shape, x.dtype) for x in scratch]]
    size = sum(4 * math.prod(x.shape) for x in held)
    fixed = smem + loose
    args = [*args[:fixed], *[pltpu.with_memory_space_constraint(x, pltpu.HBM) for x in args[fixed:]]]
    specs = [vm] * (len(args) - smem)
    for at, shape, pick in blocks:
        specs[at - smem] = pl.BlockSpec(shape, lambda i, info, *_, pick=pick: (0, info[pick]))
    got = pl.pallas_call(
        body,
        grid_spec=pltpu.PrefetchScalarGridSpec(
            num_scalar_prefetch=smem, grid=(1,), in_specs=specs, out_specs=[vm] * len(outs),
            scratch_shapes=list(scratch)),
        out_shape=[pltpu.HBM(x.shape, x.dtype) for x in outs],
        compiler_params=pltpu.CompilerParams(vmem_limit_bytes=2 * size + 8 * 1024 * 1024),
        name=name,
    )(*args)
    return tuple(got) if isinstance(out_shape, tuple) else got[0]


def sds(*shape):
    return jax.ShapeDtypeStruct(shape, F32)


def eliminate32(rows, inv_rows, lane0):
    ng = S // 8
    sub = lax.broadcasted_iota(jnp.int32, (8, T), 0)
    xa = [rows[8 * g:8 * g + 8] for g in range(ng)]
    xi = [inv_rows[8 * g:8 * g + 8] for g in range(ng)]
    def row(groups, i):
        return jnp.broadcast_to(groups[i // 8][i % 8:i % 8 + 1], (8, T))

    scale = [jnp.zeros((8, T), F32) for _ in range(ng)]
    bc = {}
    for j in range(0, S, 2):
        gj, rj = j // 8, j % 8
        end = j // G * G + G
        if j % G == 0:
            for c in range(j, end):
                bc[c] = [None] * (c // 8) + [
                    jnp.broadcast_to(xa[g][:, lane0 + c:lane0 + c + 1], (8, T)) for g in range(c // 8, ng)]
            p11, p21, p22 = row(bc[j], j), row(bc[j], j + 1), row(bc[j + 1], j + 1)
        c1, c2 = bc[j], bc[j + 1]
        det = p11 * p22 - p21 * p21
        rd = pl.reciprocal(det, approx=True)
        m1 = {c: row(c1, c) for c in range(j + 2, end)}
        m2 = {c: row(c2, c) for c in range(j + 2, end)}
        if j + 2 < end:
            a, b = j + 2, j + 3
            w1a, w2a = m1[a] * p22 - m2[a] * p21, m2[a] * p11 - m1[a] * p21
            w1b, w2b = m1[b] * p22 - m2[b] * p21, m2[b] * p11 - m1[b] * p21
            n11 = row(bc[a], a) - (w1a * m1[a] + w2a * m2[a]) * rd
            n21 = row(bc[a], b) - (w1b * m1[a] + w2b * m2[a]) * rd
            n22 = row(bc[b], b) - (w1b * m1[b] + w2b * m2[b]) * rd
        t1 = [None if g < gj else (c1[g] * p22 - c2[g] * p21) * rd for g in range(ng)]
        t2 = [None if g < gj else (c2[g] * p11 - c1[g] * p21) * rd for g in range(ng)]
        for c in range(j + 2, end):
            for g in range(c // 8, ng):
                bc[c][g] = bc[c][g] - (t1[g] * m1[c] + t2[g] * m2[c])
        r1 = lax.rsqrt(p11)
        q1 = r1 * r1
        r2 = lax.rsqrt(det * q1)
        scale[gj] = jnp.where(sub == rj, r1, jnp.where(sub == rj + 1, r2, scale[gj]))
        k1, k2 = list(t1), list(t2)
        k1[gj] = jnp.where(sub > rj + 1, t1[gj], jnp.where(sub == rj + 1, p21 * q1, 0.0))
        k2[gj] = jnp.where(sub > rj + 1, t2[gj], 0.0)
        for x in (xa, xi):
            x1, x2 = row(x, j), row(x, j + 1)
            for g in range(gj, ng):
                x[g] = x[g] - (k1[g] * x1 + k2[g] * x2)
        if j + 2 < end:
            p11, p21, p22 = n11, n21, n22
    return (
        jnp.concatenate([a * s for a, s in zip(xa, scale)], 0),
        jnp.concatenate([a * s for a, s in zip(xi, scale)], 0),
    )


def split3(x):
    h = x.astype(jnp.bfloat16)
    r = x - h.astype(F32)
    m = r.astype(jnp.bfloat16)
    return h, m, (r - m.astype(F32)).astype(jnp.bfloat16)


def factor128(a):
    r = lax.broadcasted_iota(jnp.int32, (T, T), 0)
    c = lax.broadcasted_iota(jnp.int32, (T, T), 1)
    diag = jnp.where(r == c, a, 0.0)
    across = jnp.sum(diag, axis=0, keepdims=True)
    s_row, s_col = lax.rsqrt(across), lax.rsqrt(jnp.sum(diag, axis=1, keepdims=True))
    a = a * s_row * s_col
    inv = jnp.where(r == c, 1.0, 0.0).astype(F32)
    us, ls = [], []
    for s in range(T // S):
        u, li = eliminate32(a[:S], inv[:S], s * S)
        us.append(u)
        ls.append(li)
        if s < T // S - 1:
            h, m, l = split3(u)
            hi, mi, lo = split3(li)
            left = jnp.concatenate([h, h, m, h, l, m], 0)
            right = jnp.concatenate([jnp.concatenate([x, y], 1) for x, y in
                                     ((h, hi), (m, mi), (h, hi), (l, lo), (h, hi), (m, mi))], 0)
            both = lax.dot_general(left, right, (((0,), (0,)), ((), ())), preferred_element_type=F32)
            a = a[S:] - both[(s + 1) * S:, :T]
            inv = inv[S:] - both[(s + 1) * S:, T:]
    u = jnp.concatenate(us, 0) * (across * s_row)
    return jnp.where(c >= r, u, 0.0), jnp.concatenate(ls, 0) * s_row


def factor_panel(pan, li_ref, keep=None, beside=None):
    def half(i, carry):
        d = pl.ds(pl.multiple_of(i * T, T), T)
        a = pan[d, d]
        if beside is not None:
            beside(i)
        u, li = factor128(a)
        li_ref[d, d] = li
        if keep is not None:
            keep[d, d] = u
        @pl.when(i == 0)
        def _():
            u12 = mm_nn(li, pan[:T, T:])
            pan[:T, T:] = u12
            pan[T:, T:] -= mm_tn(u12, u12)
            if keep is not None:
                keep[:T, T:] = u12
                keep[T:, :T] = jnp.zeros((T, T), F32)
        return carry
    lax.fori_loop(0, 2, half, 0)
    li_ref[:T, T:] = jnp.zeros((T, T), F32)
    li_ref[T:, :T] = -mm_nn(li_ref[T:, T:], mm_tn(pan[:T, T:], li_ref[:T, :T]))


def update_near(pan, p, us):
    for q in range(p):
        o = (p - q - 1) * Q
        pan[...] -= mm_tn(us[q][:, o:o + Q], us[q][:, o:o + Q])


def update_far(far, p, us, i):
    at = pl.ds(pl.multiple_of(i * T, T), T)
    for q in range(p):
        o = (p - q - 1) * Q
        far[at, :] -= mm_tn(us[q][:, pl.ds(pl.multiple_of(o + i * T, T), T)], us[q][:, o + Q:])


def child_kernel(p, picks, count):
    def body(info, *refs):
        got, (r_ref, t_ref), rest = refs[:count], refs[count:count + 2], refs[count + 2:]
        us, before, rest = rest[:p], rest[p:2 * p], rest[2 * p:]
        li_ref, solved = rest[:2]
        u_ref = rest[2] if p < 3 else None
        pan, x, far = rest[-3:]
        if p == 0:
            pan[...] = got[0][:, pl.ds(pl.multiple_of(info[0] * Q, Q), Q)]
            for i in range(3):
                far[:, i * Q:(i + 1) * Q] = got[0][:, pl.ds(pl.multiple_of(info[i + 1] * Q, Q), Q)]
        for z in range(4 if p else 0):
            @pl.when(info[10] == z)
            def _():
                for i, (a, lead) in enumerate(picks[z]):
                    value = got[a][...] if lead is None else got[a][lead]
                    if i == 0:
                        pan[...] = value
                    else:
                        far[:, (i - 1) * Q:i * Q] = value
        m = r_ref.shape[0]
        x[:m] = r_ref[...]
        x[m:] = t_ref[...]
        update_near(pan, p, us)
        def beside(i):
            if p < 3:
                update_far(far, p, us, i)
            n = x.shape[0] // 2
            at = pl.ds(pl.multiple_of(i * n, n), n)
            for q in range(p):
                o = (p - q - 1) * Q
                x[at, :] -= mm_nn(before[q][at, :], us[q][:, o:o + Q], THREE)
        factor_panel(pan, li_ref, None, beside if p else None)
        if p < 3:
            u_ref[...] = mm_nn(li_ref[...], far[...])
        solved[...] = mm_nt(x[...], li_ref[...], THREE)
    return body


def child_stage(p, info, got, rows, top, us, before, picks=()):
    w, n = max(1, 3 - p) * Q, rows.shape[0] + top.shape[0]
    out = (sds(Q, Q), sds(n, Q), *([sds(Q, w)] if p < 3 else []))
    k = 1 + len(got)
    return call(
        child_kernel(p, picks, len(got)), "child_panel", out, (info, *got, rows, top, *us, *before), 1,
        [vmem(Q, Q), vmem(n, Q), vmem(Q, w)], len(got) if p else 0,
        ((k, (rows.shape[0], Q), p), (k + 1, (top.shape[0], Q), p)))


def solve_rows(read, us, lis, out):
    for p in range(4):
        x = read(p)
        for q in range(p):
            o = (p - q - 1) * Q
            x = x - mm_nn(out[:, q * Q:(q + 1) * Q], us[q][:, o:o + Q], THREE)
        out[:, p * Q:(p + 1) * Q] = mm_nt(x, lis[p][...], THREE)


def pieces_kernel(info, c_ref, up, down):
    for i in range(3):
        up[i] = c_ref[:, pl.ds(pl.multiple_of(info[4 + i] * Q, Q), Q)]
        down[i] = c_ref[:, pl.ds(pl.multiple_of(info[7 + i] * Q, Q), Q)]


def top_kernel(info, cb, d1, d2, d3, p1, p2, p3, s0, s1, s2, s3, u0, u1, u2, l0, l1, l2, l3, out, cross, full, done):
    z = info[10]
    m = s0.shape[0] - T
    others = ((p1, -1), (p2, -2), (p3, -3), (d1, 1), (d2, 2), (d3, 3))
    def each(act):
        for ref, shift in others:
            at = z + shift
            slot = pl.ds(pl.multiple_of((at if shift < 0 else at - 1) * T, T), T)
            @pl.when((at >= 0) & (at < 4))
            def _():
                act(ref, pl.ds(pl.multiple_of(at * T, T), T), slot)
    def take(ref, at, slot):
        full[slot, :] = ref[...]
    def give(ref, at, slot):
        out[at, :] = done[slot, :]
    each(take)
    solve_rows(lambda p: full[:, pl.ds(pl.multiple_of(info[p] * Q, Q), Q)], (u0, u1, u2), (l0, l1, l2, l3), done)
    each(give)
    here = pl.ds(pl.multiple_of(z * T, T), T)
    for p, s in enumerate((s0, s1, s2, s3)):
        out[here, p * Q:(p + 1) * Q] = s[m:, :]
    rows = T // cross.shape[0]
    for d in range(3):
        k = lax.rem(z + d, 4)
        block = mm_nt(out[here, :], out[pl.ds(pl.multiple_of(k * T, T), T), :], THREE)
        for r in range(cross.shape[0]):
            cross[r, d * rows:(d + 1) * rows, :] = block[r * rows:(r + 1) * rows]
    which = lax.broadcasted_iota(jnp.int32, (16, T), 0)
    flags = jnp.zeros((16, T), F32)
    for k in range(4):
        flags = jnp.where(which == k, cb[0, k].astype(F32), flags)
    for r in range(cross.shape[0]):
        cross[r, 3 * rows:, :] = flags


def schur_kernel(r0, r1, r2, r3, t_ref, *refs):
    out = refs[-1]
    for k in range(4):
        at = slice(k * T, (k + 1) * T)
        out[k] = sum(mm_nt(r[...], t_ref[at, p * Q:(p + 1) * Q], THREE) for p, r in enumerate((r0, r1, r2, r3)))


def schur_half(solved, top_solved, rows, half, into=()):
    n = rows // 2
    fixed = [pltpu.with_memory_space_constraint(x, pltpu.HBM) for x in (*solved, top_solved, *into)]
    return pl.pallas_call(
        schur_kernel,
        grid=(1,),
        in_specs=[pl.BlockSpec((n, Q), lambda i: (half, 0))] * 4 + [pl.BlockSpec(memory_space=pltpu.VMEM)]
        + [pl.BlockSpec(memory_space=pl.ANY)] * len(into),
        out_specs=pl.BlockSpec((4, n, T), lambda i: (0, half, 0)),
        out_shape=pltpu.HBM((4, rows, T), F32),
        input_output_aliases={5: 0} if into else {},
        compiler_params=pltpu.CompilerParams(vmem_limit_bytes=24 * 1024 * 1024),
        name="schur",
    )(*fixed)


def strip_kernel(info, recv, base, out):
    z = info[10]
    n1, n2 = lax.rem(z + 1, 4), lax.rem(z + 2, 4)
    def start(a, k, b):
        return base[a, :, pl.ds(pl.multiple_of(k * Q + b * T, T), T)]
    out[0] = start(0, z, 0)
    out[1] = start(0, z, 1)
    out[2] = start(1, z, 1)
    for a in range(2):
        for b in range(2):
            out[3 + 2 * a + b] = start(a, n1, b)
    low = z < 2
    @pl.when(low)
    def _():
        out[7] = start(0, n2, 0)
        out[8] = start(1, n2, 0)
    @pl.when(jnp.logical_not(low))
    def _():
        out[7] = start(1, n2, 0)
        out[8] = start(1, n2, 1)
    rows = out.shape[1]
    sums = [jnp.zeros((rows, T), F32)] * 9
    first = jnp.where(low, 1.0, 0.0).astype(F32)
    for f in range(recv.shape[0]):
        def flag(k):
            return jnp.broadcast_to(recv[f, pl.ds(3 * rows + k, 1), :], (rows, T))
        a0, a1, a2 = flag(z), flag(n1), flag(n2)
        x0, x1, x2 = (recv[f, d * rows:(d + 1) * rows, :] for d in range(3))
        half = first * a0 + (1.0 - first) * a2
        kept = first * (1.0 - a2) + (1.0 - first) * a0
        places = [(0, x0, 1.0 - a0), (2, x0, a0)]
        for a in range(2):
            for b in range(2):
                places.append((3 + 2 * a + b, x1, (a0 if a else 1.0 - a0) * (a1 if b else 1.0 - a1)))
        places += [(7, x2, kept * (1.0 - half)), (8, x2, kept * half)]
        for i, x, here in places:
            sums[i] = sums[i] + jnp.where(here > 0.5, x, 0.0)
    for i in (0, 2, 3, 4, 5, 6, 7, 8):
        out[i] = out[i] - sums[i]


def nine(z):
    b, n1, n2 = 2 * z, 2 * ((z + 1) % 4), 2 * ((z + 2) % 4)
    places = [(b, b), (b, b + 1), (b + 1, b + 1)]
    places += [(b + i, n1 + j) for i in range(2) for j in range(2)]
    places += [(b, n2), (b + 1, n2)] if z < 2 else [(b + 1, n2), (b + 1, n2 + 1)]
    return [(i, j, False) if i <= j else (j, i, True) for i, j in places]


def parent_first(rels):
    def body(info, *refs):
        got = refs[:max(1, len(rels))]
        l0, keep, r1, r2, r3, u0, pan, far, tiles = refs[len(got):]
        z, f = info[10], info[11]
        if rels:
            for ref, (fs, z0) in zip(got, rels):
                rows = ref.shape[3]
                for i, rf in enumerate(fs):
                    src = jnp.bitwise_xor(f, rf)
                    for j in range(ref.shape[1]):
                        zz = jnp.bitwise_xor(z, z0 + j)
                        tiles[zz, :, pl.ds(pl.multiple_of(src * rows, rows), rows), :] = ref[i, j]
        else:
            tiles[...] = got[0][...]
        near = (pan, r1, r2, r3)
        for zz in range(4):
            for i, (r, c, turned) in enumerate(nine(zz)):
                block = tiles[zz, i]
                target, r, c = near[r // 2], r % 2, c - r // 2 * 2
                if target is pan and c >= 2:
                    target, c = far, c - 2
                target[r * T:(r + 1) * T, c * T:(c + 1) * T] = block.T if turned else block
        for target in near:
            target[T:, :T] = jnp.zeros((T, T), F32)
        factor_panel(pan, l0, keep)
        u0[...] = mm_nn(l0[...], far[...])
    return body


def parent_middle(r1, r2, u0, l1, l2, k1, k2, u1, u2, pan, far):
    us = (u0, u1)
    for p, src, li, keep, u in ((1, r1, l1, k1, u1), (2, r2, l2, k2, u2)):
        pan[...] = src[:, :Q]
        wide = far.at[:, :(3 - p) * Q]
        wide[...] = src[:, Q:]
        update_near(pan, p, us)
        factor_panel(pan, li, keep, lambda i: update_far(wide, p, us, i))
        u[...] = mm_nn(li[...], wide[...])


def own_kernel(info, u0, u1, u2, k0, k1, k2, own):
    us, keeps = (u0, u1, u2), (k0, k1, k2)
    for zz in range(4):
        @pl.when(info[10] == zz)
        def _():
            for q in range(4):
                if q < zz:
                    block = us[q][:, (zz - q - 1) * Q:(zz - q) * Q].T
                elif q == zz and zz < 3:
                    block = keeps[zz][...].T
                else:
                    block = jnp.zeros((Q, Q), F32)
                own[:, q * Q:(q + 1) * Q] = block


def last_kernel(info, r3, u0, u1, u2, _, li, corner, pan, keep):
    pan[...] = r3[...]
    update_near(pan, 3, (u0, u1, u2))
    factor_panel(pan, li, keep)
    @pl.when(info[10] == 3)
    def _():
        corner[...] = keep[...].T
    @pl.when(info[10] < 3)
    def _():
        corner[...] = jnp.zeros((Q, Q), F32)


def parent_last(info, r3, us, own):
    vm = pl.BlockSpec(memory_space=pltpu.VMEM)
    fixed = [pltpu.with_memory_space_constraint(x, pltpu.HBM) for x in (r3, *us, own)]
    return pl.pallas_call(
        last_kernel,
        grid_spec=pltpu.PrefetchScalarGridSpec(
            num_scalar_prefetch=1, grid=(1,), in_specs=[vm] * 4 + [pl.BlockSpec(memory_space=pl.ANY)],
            out_specs=[vm, pl.BlockSpec((Q, Q), lambda i, info: (0, 3))], scratch_shapes=[vmem(Q, Q), vmem(Q, Q)]),
        out_shape=[pltpu.HBM((Q, Q), F32), pltpu.HBM(own.shape, F32)],
        input_output_aliases={5: 1},
        compiler_params=pltpu.CompilerParams(vmem_limit_bytes=24 * 1024 * 1024),
        name="parent_last",
    )(info, *fixed)


def vmem(*shape):
    return pltpu.VMEM(shape, F32)


def panel_kernel(x_ref, u0, u1, u2, l0, l1, l2, l3, out):
    solve_rows(lambda p: x_ref[p], (u0, u1, u2), (l0, l1, l2, l3), out)


def pack_kernel(info, cb, owner, slot, x_ref, out):
    out[...] = jnp.zeros(out.shape, F32)
    def one(b, carry):
        o, at = owner[b], pl.ds(pl.multiple_of(slot[b] * T, T), T)
        out[o, at, :] = out[o, at, :] + x_ref[b]
        return carry
    lax.fori_loop(0, x_ref.shape[0], one, 0)
    out[:, 4 * T:, :] = jnp.full((out.shape[0], 8, T), cb[0, info[10]].astype(F32))


def land_kernel(recv, rows_ref, out):
    for s in range(4):
        at = slice(s * T, (s + 1) * T)
        def one(f, carry):
            right = jnp.broadcast_to(recv[f, 4 * T:4 * T + 1, :], (T, T)) > 0.5
            x = recv[f, at, :]
            return carry[0] - jnp.where(right, 0.0, x), carry[1] - jnp.where(right, x, 0.0)
        out[s, :, :T], out[s, :, T:] = lax.fori_loop(0, recv.shape[0], one, (rows_ref[at, :T], rows_ref[at, T:]))


def swap(x, axis, bit):
    n = lax.axis_size(axis)
    return lax.ppermute(x, axis, [(i, i ^ bit) for i in range(n)])


def everywhere(parts):
    fronts = lax.axis_size("front")
    bits = [1 << i for i in reversed(range(fronts.bit_length() - 1))]
    orders = [bits, bits[1::-1] + bits[2:]]
    got, rels = [], []
    for part, order, z0 in zip(parts, orders, (0, 2)):
        part, fs = part[None], [0]
        for bit in order[:-1]:
            part = jnp.concatenate([part, swap(part, "front", bit)], 0)
            fs = fs + [f ^ bit for f in fs]
        got += [part, swap(part, "front", order[-1])]
        rels += [(fs, z0), ([f ^ order[-1] for f in fs], z0)]
    return got, rels


def shards(
    child_diag, child_top, child_rows, row_owner, row_slot, col_block, parent_diag, parent_rows
):
    fronts = lax.axis_size("front")
    z, f = lax.axis_index("blk"), lax.axis_index("front")
    plan = lax.dynamic_slice_in_dim(jnp.array(PLAN, jnp.int32), z, 1, 0)[0]
    info = jnp.concatenate([plan, jnp.stack([z, f]).astype(jnp.int32)])
    strip_rows = T // fronts
    base = lax.dynamic_slice_in_dim(parent_diag.reshape(2, T, 4 * Q), f * strip_rows, strip_rows, 1)
    barrier = lax.optimization_barrier

    up, down = call(pieces_kernel, "pieces", (sds(3, Q, Q),) * 2, (info, child_diag), 1)
    ua1, da1 = lax.ppermute(up, "blk", UP), lax.ppermute(down, "blk", DOWN)
    l0, s0, u0 = child_stage(0, info, (child_diag,), child_rows, child_top, (), ())
    sent, l0 = barrier((child_top, l0))
    tu1, td1 = lax.ppermute(sent, "blk", UP), lax.ppermute(sent, "blk", DOWN)
    ua1, da1, l0, base = barrier((ua1, da1, l0, base))

    ua2, da2 = lax.ppermute(ua1[:2], "blk", UP[1:]), lax.ppermute(da1[:2], "blk", DOWN[:2])
    up_pick, down_pick = tuple((0, i) for i in range(3)), tuple((1, i) for i in range(3))
    l1, s1, u1 = child_stage(1, info, (ua1, da1), child_rows, child_top, (u0,), (s0,),
                             (down_pick, up_pick, down_pick, up_pick))
    ua2, da2, tu1, td1, l1 = barrier((ua2, da2, tu1, td1, l1))

    u3, d3 = lax.ppermute(ua2[0], "blk", UP[2:]), lax.ppermute(da2[0], "blk", DOWN[:1])
    tu2, td2 = lax.ppermute(tu1, "blk", UP[1:]), lax.ppermute(td1, "blk", DOWN[:2])
    l2, s2, u2 = child_stage(2, info, (da2, da1, ua1, ua2), child_rows, child_top, (u0, u1), (s0, s1),
                             tuple(((i, 0), (i, 1)) for i in range(4)))
    u3, d3, tu2, td2, l2 = barrier((u3, d3, tu2, td2, l2))

    tu3, td3 = lax.ppermute(tu2, "blk", UP[2:]), lax.ppermute(td2, "blk", DOWN[:1])
    l3, s3 = child_stage(3, info, (d3, da2, ua2, u3), child_rows, child_top, (u0, u1, u2), (s0, s1, s2),
                         (((0, None),), ((1, 0),), ((2, 0),), ((3, None),)))
    tu3, td3, l3 = barrier((tu3, td3, l3))
    top_solved, cross = call(
        top_kernel, "top_solved", (sds(4 * T, 4 * Q), sds(fronts, 3 * strip_rows + 16, T)),
        (info, col_block, td1, td2, td3, tu1, tu2, tu3, s0, s1, s2, s3, u0, u1, u2, l0, l1, l2, l3), 2,
        [vmem(3 * T, 4 * Q)] * 2, 6)

    strips = lax.all_to_all(cross, "front", 0, 0, tiled=True)
    solved, rows = (s0, s1, s2, s3), child_rows.shape[0]
    schur = schur_half(solved, top_solved, rows, 0)
    strips, schur = barrier((strips, schur))
    strip = call(strip_kernel, "diag_strip", sds(9, strip_rows, T), (info, strips, base), 1, (), 1)
    line = [swap(strip, "blk", bit) for bit in (1, 2, 3)]
    schur = schur_half(solved, top_solved, rows, 1, (schur,))
    *line, schur = barrier((*line, schur))
    if strip_rows % 8 == 0:
        got, rels = everywhere((jnp.stack([strip, line[0]]), jnp.stack(line[1:])))
    else:
        whole = lax.all_gather(strip, ("front", "blk"), axis=0).reshape(fronts, 4, 9, strip_rows, T)
        got, rels = [whole.transpose(1, 2, 0, 3, 4).reshape(4, 9, T, T)], []

    arrived = lax.all_to_all(schur, "blk", 0, 0, tiled=True)
    p0, k0, r1, r2, r3, v0 = call(
        parent_first(rels), "parent_first",
        (sds(Q, Q), sds(Q, Q), sds(Q, 3 * Q), sds(Q, 2 * Q), sds(Q, Q), sds(Q, 3 * Q)),
        (info, *got), 1, [vmem(Q, Q), vmem(Q, 3 * Q), vmem(4, 9, T, T)], len(got))
    arrived, p0, k0, r1, r2, r3, v0 = barrier((arrived, p0, k0, r1, r2, r3, v0))
    outgoing = call(pack_kernel, "outgoing", sds(fronts, 4 * T + 8, T),
                    (info, col_block, row_owner[0, :, 0], row_slot[0], arrived.reshape(-1, T, T)), 4, (), 1)
    received = lax.all_to_all(outgoing, "front", 0, 0, tiled=True)
    p1, p2, k1, k2, v1, v2 = call(
        parent_middle, "parent_middle",
        (sds(Q, Q), sds(Q, Q), sds(Q, Q), sds(Q, Q), sds(Q, 2 * Q), sds(Q, Q)), (r1, r2, v0), 0,
        [vmem(Q, Q), vmem(Q, 2 * Q)])
    own_rows = call(own_kernel, "own_rows", sds(Q, 4 * Q), (info, v0, v1, v2, k0, k1, k2), 1)
    received, p2, v2, own_rows = barrier((received, p2, v2, own_rows))
    updated = call(land_kernel, "updated", sds(4, T, Q), (received, parent_rows), 0, (), 1)
    row_major = lax.all_to_all(updated, "blk", 0, 0, tiled=True)
    p3, own_rows = parent_last(info, r3, (v0, v1, v2), own_rows)
    panel = call(panel_kernel, "parent_panel", sds(T, 4 * Q), (row_major, v0, v1, v2, p0, p1, p2, p3), 0, (), 1)
    return own_rows, panel


def solution(mesh):
    return jax.shard_map(
        shards,
        mesh=mesh,
        in_specs=(
            P(("front", "blk"), None),
            P(("front", "blk"), None),
            P(("front", "blk"), None),
            P("front", None, None),
            P("front", None),
            P("front", None),
            P("blk", None),
            P("front", "blk"),
        ),
        out_specs=(P("blk", None), P(("front", "blk"), None)),
        check_vma=False,
    )
```

```python
import math

import jax
import jax.numpy as jnp
from jax import lax
from jax.experimental import pallas as pl
from jax.experimental.pallas import tpu as pltpu
from jax.sharding import PartitionSpec as P

T = 128
S = 32
G = 16
Q = 256

PLAN = (
    (0, 1, 2, 3, 0, 2, 3, 0, 0, 0),
    (1, 0, 2, 3, 1, 0, 0, 1, 2, 3),
    (2, 3, 1, 0, 2, 1, 0, 2, 3, 3),
    (3, 2, 1, 0, 0, 0, 0, 3, 1, 0),
)
UP = ((0, 1), (1, 2), (2, 3))
DOWN = ((1, 0), (2, 1), (3, 2))
F32 = jnp.float32


def pieces_of(x, count):
    got = []
    for _ in range(count):
        got.append(x.astype(jnp.bfloat16))
        x = x - got[-1].astype(F32)
    return got


def mm(x, y, a, b, left, right):
    xs, ys = pieces_of(x, max(left) + 1), pieces_of(y, max(right) + 1)
    return lax.dot_general(
        jnp.concatenate([xs[i] for i in left], a), jnp.concatenate([ys[i] for i in right], b),
        (((a,), (b,)), ((), ())), preferred_element_type=F32)


SIX = ((0, 0, 1, 0, 2, 1), (0, 1, 0, 2, 0, 1))
THREE = ((0, 0, 1), (0, 1, 0))


def mm_nn(x, y, terms=SIX):
    return mm(x, y, 1, 0, *terms)


def mm_nt(x, y, terms=SIX):
    return mm(x, y, 1, 1, *terms)


def mm_tn(x, y, terms=SIX):
    return mm(x, y, 0, 0, *terms)


def call(body, name, out_shape, args, smem, scratch=(), loose=0, blocks=()):
    vm = pl.BlockSpec(memory_space=pltpu.VMEM)
    outs = out_shape if isinstance(out_shape, tuple) else (out_shape,)
    held = [*outs, *args, *[jax.ShapeDtypeStruct(x.shape, x.dtype) for x in scratch]]
    size = sum(4 * math.prod(x.shape) for x in held)
    fixed = smem + loose
    args = [*args[:fixed], *[pltpu.with_memory_space_constraint(x, pltpu.HBM) for x in args[fixed:]]]
    specs = [vm] * (len(args) - smem)
    for at, shape, pick in blocks:
        specs[at - smem] = pl.BlockSpec(shape, pick)
    got = pl.pallas_call(
        body,
        grid_spec=pltpu.PrefetchScalarGridSpec(
            num_scalar_prefetch=smem, grid=(1,), in_specs=specs, out_specs=[vm] * len(outs),
            scratch_shapes=list(scratch)),
        out_shape=[pltpu.HBM(x.shape, x.dtype) for x in outs],
        compiler_params=pltpu.CompilerParams(vmem_limit_bytes=2 * size + 8 * 1024 * 1024),
        name=name,
    )(*args)
    return tuple(got) if isinstance(out_shape, tuple) else got[0]


def sds(*shape):
    return jax.ShapeDtypeStruct(shape, F32)


def eliminate32(rows, inv_rows, lane0):
    ng = S // 8
    sub = lax.broadcasted_iota(jnp.int32, (8, T), 0)
    xa = [rows[8 * g:8 * g + 8] for g in range(ng)]
    xi = [inv_rows[8 * g:8 * g + 8] for g in range(ng)]
    def row(groups, i):
        return jnp.broadcast_to(groups[i // 8][i % 8:i % 8 + 1], (8, T))

    scale = [jnp.zeros((8, T), F32) for _ in range(ng)]
    bc = {}
    for j in range(0, S, 2):
        gj, rj = j // 8, j % 8
        end = j // G * G + G
        if j % G == 0:
            for c in range(j, end):
                bc[c] = [None] * (c // 8) + [
                    jnp.broadcast_to(xa[g][:, lane0 + c:lane0 + c + 1], (8, T)) for g in range(c // 8, ng)]
            p11, p21, p22 = row(bc[j], j), row(bc[j], j + 1), row(bc[j + 1], j + 1)
        c1, c2 = bc[j], bc[j + 1]
        det = p11 * p22 - p21 * p21
        rd = pl.reciprocal(det, approx=True)
        m1 = {c: row(c1, c) for c in range(j + 2, end)}
        m2 = {c: row(c2, c) for c in range(j + 2, end)}
        if j + 2 < end:
            a, b = j + 2, j + 3
            w1a, w2a = m1[a] * p22 - m2[a] * p21, m2[a] * p11 - m1[a] * p21
            w1b, w2b = m1[b] * p22 - m2[b] * p21, m2[b] * p11 - m1[b] * p21
            n11 = row(bc[a], a) - (w1a * m1[a] + w2a * m2[a]) * rd
            n21 = row(bc[a], b) - (w1b * m1[a] + w2b * m2[a]) * rd
            n22 = row(bc[b], b) - (w1b * m1[b] + w2b * m2[b]) * rd
        t1 = [None if g < gj else (c1[g] * p22 - c2[g] * p21) * rd for g in range(ng)]
        t2 = [None if g < gj else (c2[g] * p11 - c1[g] * p21) * rd for g in range(ng)]
        for c in range(j + 2, end):
            for g in range(c // 8, ng):
                bc[c][g] = bc[c][g] - (t1[g] * m1[c] + t2[g] * m2[c])
        r1 = lax.rsqrt(p11)
        q1 = r1 * r1
        r2 = lax.rsqrt(det * q1)
        scale[gj] = jnp.where(sub == rj, r1, jnp.where(sub == rj + 1, r2, scale[gj]))
        k1, k2 = list(t1), list(t2)
        k1[gj] = jnp.where(sub > rj + 1, t1[gj], jnp.where(sub == rj + 1, p21 * q1, 0.0))
        k2[gj] = jnp.where(sub > rj + 1, t2[gj], 0.0)
        for x in (xa, xi):
            x1, x2 = row(x, j), row(x, j + 1)
            for g in range(gj, ng):
                x[g] = x[g] - (k1[g] * x1 + k2[g] * x2)
        if j + 2 < end:
            p11, p21, p22 = n11, n21, n22
    return (
        jnp.concatenate([a * s for a, s in zip(xa, scale)], 0),
        jnp.concatenate([a * s for a, s in zip(xi, scale)], 0),
    )


def split3(x):
    h = x.astype(jnp.bfloat16)
    r = x - h.astype(F32)
    m = r.astype(jnp.bfloat16)
    return h, m, (r - m.astype(F32)).astype(jnp.bfloat16)


def factor128(a):
    r = lax.broadcasted_iota(jnp.int32, (T, T), 0)
    c = lax.broadcasted_iota(jnp.int32, (T, T), 1)
    diag = jnp.where(r == c, a, 0.0)
    across = jnp.sum(diag, axis=0, keepdims=True)
    s_row, s_col = lax.rsqrt(across), lax.rsqrt(jnp.sum(diag, axis=1, keepdims=True))
    a = a * s_row * s_col
    inv = jnp.where(r == c, 1.0, 0.0).astype(F32)
    us, ls = [], []
    for s in range(T // S):
        u, li = eliminate32(a[:S], inv[:S], s * S)
        us.append(u)
        ls.append(li)
        if s < T // S - 1:
            h, m, l = split3(u)
            hi, mi, lo = split3(li)
            left = jnp.concatenate([h, h, m, h, l, m], 0)
            right = jnp.concatenate([jnp.concatenate([x, y], 1) for x, y in
                                     ((h, hi), (m, mi), (h, hi), (l, lo), (h, hi), (m, mi))], 0)
            both = lax.dot_general(left, right, (((0,), (0,)), ((), ())), preferred_element_type=F32)
            a = a[S:] - both[(s + 1) * S:, :T]
            inv = inv[S:] - both[(s + 1) * S:, T:]
    u = jnp.concatenate(us, 0) * (across * s_row)
    return jnp.where(c >= r, u, 0.0), jnp.concatenate(ls, 0) * s_row


def factor_panel(pan, li_ref, keep=None, beside=None):
    def half(i, carry):
        d = pl.ds(pl.multiple_of(i * T, T), T)
        a = pan[d, d]
        if beside is not None:
            beside(i)
        u, li = factor128(a)
        li_ref[d, d] = li
        if keep is not None:
            keep[d, d] = u
        @pl.when(i == 0)
        def _():
            u12 = mm_nn(li, pan[:T, T:])
            pan[:T, T:] = u12
            pan[T:, T:] -= mm_tn(u12, u12)
            if keep is not None:
                keep[:T, T:] = u12
                keep[T:, :T] = jnp.zeros((T, T), F32)
        return carry
    lax.fori_loop(0, 2, half, 0)
    li_ref[:T, T:] = jnp.zeros((T, T), F32)
    li_ref[T:, :T] = -mm_nn(li_ref[T:, T:], mm_tn(pan[:T, T:], li_ref[:T, :T]))


def update_near(pan, p, us):
    for q in range(p):
        o = (p - q - 1) * Q
        pan[...] -= mm_tn(us[q][:, o:o + Q], us[q][:, o:o + Q])


def update_far(far, p, us, i):
    at = pl.ds(pl.multiple_of(i * T, T), T)
    for q in range(p):
        o = (p - q - 1) * Q
        far[at, :] -= mm_tn(us[q][:, pl.ds(pl.multiple_of(o + i * T, T), T)], us[q][:, o + Q:])


def child_kernel(p, picks, count):
    def body(info, *refs):
        got, (r_ref, t_ref), rest = refs[:count], refs[count:count + 2], refs[count + 2:]
        us, before, rest = rest[:p], rest[p:2 * p], rest[2 * p:]
        li_ref, solved = rest[:2]
        u_ref = rest[2] if p < 3 else None
        pan, x, far = rest[-3:]
        if p == 0:
            pan[...] = got[0][:, pl.ds(pl.multiple_of(info[0] * Q, Q), Q)]
            for i in range(3):
                far[:, i * Q:(i + 1) * Q] = got[0][:, pl.ds(pl.multiple_of(info[i + 1] * Q, Q), Q)]
        for z in range(4 if p else 0):
            @pl.when(info[10] == z)
            def _():
                for i, (r, c) in enumerate(SENT[:15 - 4 * p]):
                    target, at = (pan, c) if c < 2 else (far, c - 2)
                    target[r * T:(r + 1) * T, at * T:(at + 1) * T] = got[picks[z]][i]
        if p:
            pan[T:, :T] = jnp.zeros((T, T), F32)
        m = r_ref.shape[0]
        x[:m] = r_ref[...]
        x[m:] = t_ref[...]
        update_near(pan, p, us)
        def beside(i):
            if p < 3:
                update_far(far, p, us, i)
            n = x.shape[0] // 2
            at = pl.ds(pl.multiple_of(i * n, n), n)
            for q in range(p):
                o = (p - q - 1) * Q
                x[at, :] -= mm_nn(before[q][at, :], us[q][:, o:o + Q], THREE)
        factor_panel(pan, li_ref, None, beside if p else None)
        if p < 3:
            u_ref[...] = mm_nn(li_ref[...], far[...])
        solved[...] = mm_nt(x[...], li_ref[...], THREE)
    return body


def child_stage(p, info, got, rows, top, us, before, picks=()):
    w, n = max(1, 3 - p) * Q, rows.shape[0] + top.shape[0]
    out = (sds(Q, Q), sds(n, Q), *([sds(Q, w)] if p < 3 else []))
    k = 1 + len(got)
    def pick(i, info):
        return 0, info[p]
    return call(
        child_kernel(p, picks, len(got)), "child_panel", out, (info, *got, rows, top, *us, *before), 1,
        [vmem(Q, Q), vmem(n, Q), vmem(Q, w)], len(got) if p else 0,
        ((k, (rows.shape[0], Q), pick), (k + 1, (top.shape[0], Q), pick)))


def solve_rows(read, us, lis, out):
    for p in range(4):
        x = read(p)
        for q in range(p):
            o = (p - q - 1) * Q
            x = x - mm_nn(out[:, q * Q:(q + 1) * Q], us[q][:, o:o + Q], THREE)
        out[:, p * Q:(p + 1) * Q] = mm_nt(x, lis[p][...], THREE)


SENT = ((0, 0), (0, 1), (1, 1)) + tuple((r, c) for q in (1, 2) for r in (0, 1) for c in (2 * q, 2 * q + 1))


def pieces_kernel(info, c_ref, up, down):
    for out, first in ((up, 4), (down, 7)):
        for i, (r, c) in enumerate(SENT):
            at = pl.multiple_of(info[first + c // 2] * Q, Q) + c % 2 * T
            out[i] = c_ref[r * T:(r + 1) * T, pl.ds(at, T)]


def top_kernel(info, cb, d1, d2, d3, p1, p2, p3, s0, s1, s2, s3, u0, u1, u2, l0, l1, l2, l3, out, cross, full, done):
    z = info[10]
    others = ((p1, -1), (p2, -2), (p3, -3), (d1, 1), (d2, 2), (d3, 3))
    def each(act):
        for ref, shift in others:
            at = z + shift
            slot = pl.ds(pl.multiple_of((at if shift < 0 else at - 1) * T, T), T)
            @pl.when((at >= 0) & (at < 4))
            def _():
                act(ref, pl.ds(pl.multiple_of(at * T, T), T), slot)
    def take(ref, at, slot):
        full[slot, :] = ref[...]
    def give(ref, at, slot):
        out[at, :] = done[slot, :]
    each(take)
    solve_rows(lambda p: full[:, pl.ds(pl.multiple_of(info[p] * Q, Q), Q)], (u0, u1, u2), (l0, l1, l2, l3), done)
    each(give)
    here = pl.ds(pl.multiple_of(z * T, T), T)
    for p, s in enumerate((s0, s1, s2, s3)):
        out[here, p * Q:(p + 1) * Q] = s[...]
    rows = T // cross.shape[0]
    done_blocks = 0
    for k in range(4):
        wide = mm_nt(out[k * T:(k + 1) * T, :], out[k * T:, :], THREE)
        for i in range(4 - k):
            t = done_blocks * rows
            for r in range(cross.shape[0]):
                cross[r, t:t + rows, :] = wide[r * rows:(r + 1) * rows, i * T:(i + 1) * T]
            done_blocks += 1
    which = lax.broadcasted_iota(jnp.int32, (16, T), 0)
    flags = jnp.zeros((16, T), F32)
    for k in range(4):
        flags = jnp.where(which == k, cb[0, k].astype(F32), flags)
    for r in range(cross.shape[0]):
        cross[r, 10 * rows:, :] = flags


def schur_kernel(r0, r1, r2, r3, t_ref, out):
    for k in range(4):
        at = slice(k * T, (k + 1) * T)
        out[k] = sum(mm_nt(r[...], t_ref[at, p * Q:(p + 1) * Q], THREE) for p, r in enumerate((r0, r1, r2, r3)))


def schur_blocks(solved, top_solved, rows):
    fixed = [pltpu.with_memory_space_constraint(x, pltpu.HBM) for x in (*solved, top_solved)]
    return pl.pallas_call(
        schur_kernel,
        grid=(1,),
        in_specs=[pl.BlockSpec((rows, Q), lambda i: (0, 0))] * 4 + [pl.BlockSpec(memory_space=pltpu.VMEM)],
        out_specs=pl.BlockSpec((4, rows, T), lambda i: (0, 0, 0)),
        out_shape=pltpu.HBM((4, rows, T), F32),
        compiler_params=pltpu.CompilerParams(vmem_limit_bytes=24 * 1024 * 1024),
        name="schur",
    )(*fixed)


UPPER = [(r, c) for r in range(8) for c in range(r, 8)]


def strip_kernel(info, recv, b0, b1, b2, b3, out, base):
    z = info[10]
    for i, ref in enumerate((b0, b1, b2, b3)):
        base[jnp.bitwise_xor(z, i)] = ref[...]
    rows = out.shape[1]
    sums = {at: jnp.zeros((rows, T), F32) for at in UPPER}
    for f in range(recv.shape[0]):
        flags = [jnp.broadcast_to(recv[f, 10 * rows + k:10 * rows + k + 1, :], (rows, T)) for k in range(4)]
        sides = [(1.0 - a, a) for a in flags]
        t = 0
        for k in range(4):
            for l in range(k, 4):
                x = recv[f, t * rows:(t + 1) * rows, :]
                t += 1
                for i in range(2):
                    for j in range(2):
                        if k == l and i != j:
                            continue
                        at = (2 * k + i, 2 * l + j)
                        sums[at] = sums[at] + jnp.where(sides[k][i] * sides[l][j] > 0.5, x, 0.0)
    for i, (r, c) in enumerate(UPPER):
        out[i] = base[r // 2, r % 2, :, c * T:(c + 1) * T] - sums[r, c]


def parent_first(rels):
    def body(info, *refs):
        got = refs[:max(1, len(rels))]
        l0, keep, r1, r2, r3, u0, pan, far = refs[len(got):]
        near = (pan, r1, r2, r3)
        def place(i, start, rows, value):
            r, c = UPPER[i]
            target, r, c = near[r // 2], r % 2, c - r // 2 * 2
            if target is pan and c >= 2:
                target, c = far, c - 2
            target[pl.ds(pl.multiple_of(r * T + start, 8), rows), c * T:(c + 1) * T] = value
        for ref, (fs, first) in zip(got, rels):
            rows = ref.shape[2]
            for i, rf in enumerate(fs):
                start = jnp.bitwise_xor(info[11], rf) * rows
                for t in range(ref.shape[1]):
                    place(first + t, start, rows, ref[i, t])
        if not rels:
            for t in range(len(UPPER)):
                place(t, 0, T, got[0][t])
        for target in near:
            target[T:, :T] = jnp.zeros((T, T), F32)
        factor_panel(pan, l0, keep)
        u0[...] = mm_nn(l0[...], far[...])
    return body


def parent_middle(r1, r2, u0, l1, l2, k1, k2, u1, u2, pan, far):
    us = (u0, u1)
    for p, src, li, keep, u in ((1, r1, l1, k1, u1), (2, r2, l2, k2, u2)):
        pan[...] = src[:, :Q]
        wide = far.at[:, :(3 - p) * Q]
        wide[...] = src[:, Q:]
        update_near(pan, p, us)
        factor_panel(pan, li, keep, lambda i: update_far(wide, p, us, i))
        u[...] = mm_nn(li[...], wide[...])


def own_kernel(info, u0, u1, u2, k0, k1, k2, own):
    us, keeps = (u0, u1, u2), (k0, k1, k2)
    for zz in range(4):
        @pl.when(info[10] == zz)
        def _():
            for q in range(4):
                if q < zz:
                    block = us[q][:, (zz - q - 1) * Q:(zz - q) * Q].T
                elif q == zz and zz < 3:
                    block = keeps[zz][...].T
                else:
                    block = jnp.zeros((Q, Q), F32)
                own[:, q * Q:(q + 1) * Q] = block


def last_kernel(info, r3, u0, u1, u2, _, li, corner, pan, keep):
    pan[...] = r3[...]
    update_near(pan, 3, (u0, u1, u2))
    factor_panel(pan, li, keep)
    @pl.when(info[10] == 3)
    def _():
        corner[...] = keep[...].T
    @pl.when(info[10] < 3)
    def _():
        corner[...] = jnp.zeros((Q, Q), F32)


def parent_last(info, r3, us, own):
    vm = pl.BlockSpec(memory_space=pltpu.VMEM)
    fixed = [pltpu.with_memory_space_constraint(x, pltpu.HBM) for x in (r3, *us, own)]
    return pl.pallas_call(
        last_kernel,
        grid_spec=pltpu.PrefetchScalarGridSpec(
            num_scalar_prefetch=1, grid=(1,), in_specs=[vm] * 4 + [pl.BlockSpec(memory_space=pl.ANY)],
            out_specs=[vm, pl.BlockSpec((Q, Q), lambda i, info: (0, 3))], scratch_shapes=[vmem(Q, Q), vmem(Q, Q)]),
        out_shape=[pltpu.HBM((Q, Q), F32), pltpu.HBM(own.shape, F32)],
        input_output_aliases={5: 1},
        compiler_params=pltpu.CompilerParams(vmem_limit_bytes=24 * 1024 * 1024),
        name="parent_last",
    )(info, *fixed)


def vmem(*shape):
    return pltpu.VMEM(shape, F32)


def panel_kernel(x_ref, u0, u1, u2, l0, l1, l2, l3, out):
    solve_rows(lambda p: x_ref[p], (u0, u1, u2), (l0, l1, l2, l3), out)


def pack_kernel(info, cb, owner, slot, x_ref, out):
    out[...] = jnp.zeros(out.shape, F32)
    def one(b, carry):
        o, at = owner[b], pl.ds(pl.multiple_of(slot[b] * T, T), T)
        out[o, at, :] = out[o, at, :] + x_ref[b]
        return carry
    lax.fori_loop(0, x_ref.shape[0], one, 0)
    out[:, 4 * T:, :] = jnp.full((out.shape[0], 8, T), cb[0, info[10]].astype(F32))


def land_kernel(recv, rows_ref, out):
    for s in range(4):
        at = slice(s * T, (s + 1) * T)
        def one(f, carry):
            right = jnp.broadcast_to(recv[f, 4 * T:4 * T + 1, :], (T, T)) > 0.5
            x = recv[f, at, :]
            return carry[0] - jnp.where(right, 0.0, x), carry[1] - jnp.where(right, x, 0.0)
        out[s, :, :T], out[s, :, T:] = lax.fori_loop(0, recv.shape[0], one, (rows_ref[at, :T], rows_ref[at, T:]))


def swap(x, axis, bit):
    n = lax.axis_size(axis)
    return lax.ppermute(x, axis, [(i, i ^ bit) for i in range(n)])


def everywhere(strip):
    fronts = lax.axis_size("front")
    half = strip.shape[0] // 2
    bits = [1 << i for i in reversed(range(fronts.bit_length() - 1))]
    orders = [bits, bits[1::-1] + bits[2:]]
    got, rels = [], []
    for part, order, first in zip((strip[:half], strip[half:]), orders, (0, half)):
        part, fs = part[None], [0]
        for bit in order[:-1]:
            part = jnp.concatenate([part, swap(part, "front", bit)], 0)
            fs = fs + [f ^ bit for f in fs]
        got += [part, swap(part, "front", order[-1])]
        rels += [(fs, first), ([f ^ order[-1] for f in fs], first)]
    return got, rels


def shards(
    child_diag, child_top, child_rows, row_owner, row_slot, col_block, parent_diag, parent_rows
):
    fronts = lax.axis_size("front")
    z, f = lax.axis_index("blk"), lax.axis_index("front")
    plan = lax.dynamic_slice_in_dim(jnp.array(PLAN, jnp.int32), z, 1, 0)[0]
    info = jnp.concatenate([plan, jnp.stack([z, f]).astype(jnp.int32)])
    strip_rows = T // fronts
    base = lax.dynamic_slice_in_dim(parent_diag.reshape(2, T, 4 * Q), f * strip_rows, strip_rows, 1)
    barrier = lax.optimization_barrier

    up, down = call(pieces_kernel, "pieces", (sds(11, T, T),) * 2, (info, child_diag), 1)
    ua1, da1 = lax.ppermute(up, "blk", UP), lax.ppermute(down, "blk", DOWN)
    l0, s0, u0 = child_stage(0, info, (child_diag,), child_rows, child_top, (), ())
    sent, l0 = barrier((child_top, l0))
    tu1, td1 = lax.ppermute(sent, "blk", UP), lax.ppermute(sent, "blk", DOWN)
    ua1, da1, l0, base = barrier((ua1, da1, l0, base))

    ua2, da2 = lax.ppermute(ua1[:7], "blk", UP[1:]), lax.ppermute(da1[:7], "blk", DOWN[:2])
    l1, s1, u1 = child_stage(1, info, (ua1, da1), child_rows, child_top, (u0,), (s0,),
                             (1, 0, 1, 0))
    ua2, da2, tu1, td1, l1 = barrier((ua2, da2, tu1, td1, l1))

    u3, d3 = lax.ppermute(ua2[:3], "blk", UP[2:]), lax.ppermute(da2[:3], "blk", DOWN[:1])
    tu2, td2 = lax.ppermute(tu1, "blk", UP[1:]), lax.ppermute(td1, "blk", DOWN[:2])
    l2, s2, u2 = child_stage(2, info, (da2, da1, ua1, ua2), child_rows, child_top, (u0, u1), (s0, s1),
                             (0, 1, 2, 3))
    u3, d3, tu2, td2, l2 = barrier((u3, d3, tu2, td2, l2))

    tu3, td3 = lax.ppermute(tu2, "blk", UP[2:]), lax.ppermute(td2, "blk", DOWN[:1])
    l3, s3 = child_stage(3, info, (d3, da2, ua2, u3), child_rows, child_top, (u0, u1, u2), (s0, s1, s2),
                         (0, 1, 2, 3))
    tu3, td3, l3, base = barrier((tu3, td3, l3, base))
    bases = [base, *[swap(base, "blk", bit) for bit in (1, 2, 3)]]
    top_solved, cross = call(
        top_kernel, "top_solved", (sds(4 * T, 4 * Q), sds(fronts, 10 * strip_rows + 16, T)),
        (info, col_block, td1, td2, td3, tu1, tu2, tu3, s0, s1, s2, s3, u0, u1, u2, l0, l1, l2, l3), 2,
        [vmem(3 * T, 4 * Q)] * 2, 6,
        tuple((8 + i, (T, Q), lambda i, *_: (child_rows.shape[0] // T, 0)) for i in range(4)))

    cross, top_solved, *bases = barrier((cross, top_solved, *bases))
    strips = lax.all_to_all(cross, "front", 0, 0, tiled=True)
    schur = schur_blocks((s0, s1, s2, s3), top_solved, child_rows.shape[0])
    strips, schur = barrier((strips, schur))
    strip = call(strip_kernel, "diag_strip", sds(36, strip_rows, T), (info, strips, *bases), 1,
                 [vmem(4, 2, strip_rows, 4 * Q)], 5)
    if strip_rows % 8 == 0:
        got, rels = everywhere(strip)
    else:
        whole = lax.all_gather(strip, "front", axis=0)
        got, rels = [whole.transpose(1, 0, 2, 3).reshape(36, T, T)], []

    arrived = lax.all_to_all(schur, "blk", 0, 0, tiled=True)
    p0, k0, r1, r2, r3, v0 = call(
        parent_first(rels), "parent_first",
        (sds(Q, Q), sds(Q, Q), sds(Q, 3 * Q), sds(Q, 2 * Q), sds(Q, Q), sds(Q, 3 * Q)),
        (info, *got), 1, [vmem(Q, Q), vmem(Q, 3 * Q)], len(got))
    arrived, p0, k0, r1, r2, r3, v0 = barrier((arrived, p0, k0, r1, r2, r3, v0))
    outgoing = call(pack_kernel, "outgoing", sds(fronts, 4 * T + 8, T),
                    (info, col_block, row_owner[0, :, 0], row_slot[0], arrived.reshape(-1, T, T)), 4, (), 1)
    received = lax.all_to_all(outgoing, "front", 0, 0, tiled=True)
    p1, p2, k1, k2, v1, v2 = call(
        parent_middle, "parent_middle",
        (sds(Q, Q), sds(Q, Q), sds(Q, Q), sds(Q, Q), sds(Q, 2 * Q), sds(Q, Q)), (r1, r2, v0), 0,
        [vmem(Q, Q), vmem(Q, 2 * Q)])
    own_rows = call(own_kernel, "own_rows", sds(Q, 4 * Q), (info, v0, v1, v2, k0, k1, k2), 1)
    received, p2, v2, own_rows = barrier((received, p2, v2, own_rows))
    updated = call(land_kernel, "updated", sds(4, T, Q), (received, parent_rows), 0, (), 1)
    row_major = lax.all_to_all(updated, "blk", 0, 0, tiled=True)
    p3, own_rows = parent_last(info, r3, (v0, v1, v2), own_rows)
    panel = call(panel_kernel, "parent_panel", sds(T, 4 * Q), (row_major, v0, v1, v2, p0, p1, p2, p3), 0, (), 1)
    return own_rows, panel


def solution(mesh):
    return jax.shard_map(
        shards,
        mesh=mesh,
        in_specs=(
            P(("front", "blk"), None),
            P(("front", "blk"), None),
            P(("front", "blk"), None),
            P("front", None, None),
            P("front", None),
            P("front", None),
            P("blk", None),
            P("front", "blk"),
        ),
        out_specs=(P("blk", None), P(("front", "blk"), None)),
        check_vma=False,
    )
```
